256 devices in a mesh: dp: 16 (over y, x_lo, core), sp: 16 (over z, x_hi).
Axes of the slice: x: 4 (x_hi: 2, x_lo: 2; x = x_hi * 2 + x_lo), y: 4, z: 8, core: 2. Of those that a mesh axis runs over, the one named last changes fastest.
Arguments:
- query: bfloat16 [16, 2048, 2048], P('dp', 'sp'), may hold values from -6 to 6
- key_in: bfloat16 [16, 2048, 2048], P('dp', 'sp'), may hold values from -6 to 6
- value: bfloat16 [16, 2048, 2048], P('dp', 'sp'), may hold values from -6 to 6
- bucket: int32 [16], P('dp'), may hold values from 0 to 1, as said below
- clip_cost: int32 [16, 4], P('dp'), may hold values from 0 to 999
- positions: int32 [3, 16, 2048], P(None, 'dp', 'sp'), may hold values from 0 to 63
- out_weight: bfloat16 [2048, 3072], P('sp'), may hold values from -0.125 to 0.125
- cotangent: bfloat16 [16, 2048, 3072], P('dp', 'sp'), may hold values from -6 to 6
Outputs:
- mixed: bfloat16 [16, 2048, 3072], P('dp', 'sp')
- grad_query: bfloat16 [16, 2048, 2048], P('dp', 'sp')
- grad_key: bfloat16 [16, 2048, 2048], P('dp', 'sp')
- grad_value: bfloat16 [16, 2048, 2048], P('dp', 'sp')
- grad_weight: float32 [2048, 3072], P('sp', 'dp')
The draws below stay inside these ranges and needn't reach their ends.
Inputs may be any that keep to these rules, and one draw needn't show every extreme that they name: Exactly half of the rows have bucket 1.
All inputs are finite; a program needn't handle non-finite values.
Results may differ from the reference program's by a relative error of at most 0.023.
Values may be sent and summed in bfloat16 or wider, within the bound.
A program may use at most 128 MiB of HBM per device.

```python
import jax
import jax.numpy as jnp
import numpy as np
from jax import lax

D = 3072
HEADS = 16
HD = 128
CLIPS = 4
GROUP = 2048
INNER = 2048
N_DP = 16


def draw_query(key, part):
    key = jax.random.fold_in(key, 21)
    shape = (N_DP, GROUP, HEADS * HD)
    values = jnp.clip(jax.random.normal(key, shape), -6.0, 6.0)
    return values.astype(jnp.bfloat16)


def draw_key_in(key, part):
    key = jax.random.fold_in(key, 22)
    shape = (N_DP, GROUP, HEADS * HD)
    values = jnp.clip(jax.random.normal(key, shape), -6.0, 6.0)
    return values.astype(jnp.bfloat16)


def draw_bucket(key, part):
    key = jax.random.fold_in(key, 31)
    order = jax.random.permutation(key, N_DP)
    return (order < N_DP // 2).astype(jnp.int32)


def place_ends(values, rng, low, high):
    place = [jax.random.randint(jax.random.fold_in(rng, axis), (), 0, length) for axis, length in enumerate(values.shape)]
    widest = values.shape.index(max(values.shape))
    neighbour = place[:widest] + [(place[widest] + 1) % values.shape[widest]] + place[widest + 1:]
    return values.at[tuple(place)].set(low).at[tuple(neighbour)].set(high)


def strengthened(values, own_key, source, target, blocks, factor):
    def block_of(axis_at):
        return (jnp.arange(values.shape[axis_at]) // (values.shape[axis_at] // blocks)).reshape((-1,) + (1,) * (values.ndim - 1 - axis_at))

    one_side = jax.random.permutation(own_key, blocks)[block_of(target)]
    second = (block_of(target) + blocks // 2) % blocks
    return jnp.where((block_of(source) == one_side) | (block_of(source) == second), factor * values, values)


def steps_of(stream_key, shape, shards, least, high):
    def one(position, shards_of):
        draws = jax.random.uniform(jax.random.fold_in(jax.random.fold_in(stream_key, 6), position), (shards_of,), jnp.float32, least / len(shards), high / len(shards))
        return jnp.repeat(jnp.exp(draws), shape[position] // shards_of).reshape((-1,) + (1,) * (len(shape) - position - 1))

    factor_of = one(*shards[0])
    for cut in shards[1:]:
        factor_of = factor_of * one(*cut)
    return factor_of


def gaussian(stream_key, dims, spread, limit, pieces=(), kind=jnp.bfloat16):
    result = spread * jax.random.normal(stream_key, dims, jnp.float32)
    if pieces:
        result = result * steps_of(stream_key, dims, pieces, -0.22, 0.18)
    return jnp.clip(result, -limit, limit).astype(kind)


def noise_with(stream_key, dims, scale, limit, cuts, heavy, kind=jnp.bfloat16):
    values = scale * jax.random.normal(stream_key, dims, jnp.float32)
    if cuts:
        values = values * steps_of(stream_key, dims, cuts, -0.22, 0.18)
    return jnp.clip(strengthened(values, jax.random.fold_in(stream_key, 3), *heavy), -limit, limit).astype(kind)


def setup_inputs(seed: int = 0) -> dict:
    splits = jax.random.split(jax.random.key(seed), 9)
    return {
        "query": draw_query(jax.random.fold_in(splits[8], 71), 0),
        "key_in": draw_key_in(jax.random.fold_in(splits[8], 71), 0),
        "value": gaussian(splits[2], (N_DP, GROUP, INNER), 1.0, 6.0, ((0, 16), (1, 16))),
        "bucket": draw_bucket(jax.random.fold_in(splits[8], 71), 0),
        "clip_cost": place_ends(jax.random.randint(splits[4], (N_DP, CLIPS), 0, 1000), jax.random.fold_in(splits[4], 1), 0, 999).astype(jnp.int32),
        "positions": place_ends(jax.random.randint(splits[5], (3, N_DP, GROUP), 0, 64), jax.random.fold_in(splits[5], 1), 0, 63).astype(jnp.int32),
        "out_weight": gaussian(splits[6], (INNER, D), INNER ** -0.5, 0.125, ((0, 16),)),
        "cotangent": noise_with(splits[7], (N_DP, GROUP, D), 1.0, 6.0, ((0, 16), (1, 16)), (0, 2, 16, 2.0)),
    }


def rotary_layout(head_dim):
    quarter = head_dim // 4
    rest_span = (head_dim - quarter) // 2
    part_spans = (quarter, rest_span, head_dim - quarter - rest_span)
    partner = []
    signs = []
    axis_of = []
    frequency = []
    offset = 0
    for part_index in range(3):
        part_span = part_spans[part_index]
        half_span = part_span // 2
        for inner_dim in range(part_span):
            pair_index = inner_dim % half_span
            if inner_dim < half_span:
                partner.append(offset + inner_dim + half_span)
                signs.append(-1.0)
            else:
                partner.append(offset + inner_dim - half_span)
                signs.append(1.0)
            axis_of.append(part_index)
            frequency.append(10000.0 ** (-pair_index / half_span))
        offset += part_span
    return np.array(partner), np.array(signs), np.array(axis_of), np.array(frequency)


def rotary_tables(places, head_dim):
    partner, signs, axis_of, frequency = rotary_layout(head_dim)
    angles = jnp.transpose(places.astype(jnp.float32)[axis_of]) * jnp.asarray(frequency, jnp.float32)[None, :]
    return jnp.cos(angles), jnp.sin(angles) * jnp.asarray(signs, jnp.float32)[None, :]


def spin(flat, cosine, sine_signed, direction, head_dim):
    partner = rotary_layout(head_dim)[0]
    count = flat.shape[0]
    values = flat.astype(jnp.float32).reshape(count, -1, head_dim)
    turned = values * cosine[:, None, :] + direction * values[..., partner] * sine_signed[:, None, :]
    return turned.reshape(count, -1)


def deal_tables(costs, wide):
    slots = jnp.arange(costs.shape[0], dtype=jnp.int32)
    above = (costs[None, :] > costs[:, None]) | ((costs[None, :] == costs[:, None]) & (slots[None, :] < slots[:, None]))
    rank = jnp.sum(above.astype(jnp.int32), axis=1).astype(jnp.int32)
    order = jnp.sum(jnp.where(rank[None, :] == slots[:, None], slots[None, :], 0), axis=1).astype(jnp.int32)
    rank = jnp.where(wide == 1, slots, rank).astype(jnp.int32)
    order = jnp.where(wide == 1, slots, order).astype(jnp.int32)
    return rank, order


def take_blocks(rows, index):
    count = rows.shape[0]
    blocks = rows.reshape(index.shape[0], count // index.shape[0], -1)
    return jnp.take(blocks, index, axis=0).reshape(count, -1)


def head_pass(query_h, key_h, value_h, grad_h, clip_row):
    factor = HD ** -0.5
    scores = jnp.dot(query_h, key_h.T, preferred_element_type=jnp.float32) * factor
    scores = jnp.where(clip_row[:, None] == clip_row[None, :], scores, -1e30)
    top = jnp.max(scores, axis=1, keepdims=True)
    raw_weights = jnp.exp(scores - top)
    probs = raw_weights / jnp.sum(raw_weights, axis=1, keepdims=True)
    probs_low = probs.astype(jnp.bfloat16)
    attended = jnp.dot(probs_low, value_h, preferred_element_type=jnp.float32).astype(jnp.bfloat16)
    grad_probs = jnp.dot(grad_h, value_h.T, preferred_element_type=jnp.float32)
    centre = jnp.sum(probs * grad_probs, axis=1, keepdims=True)
    grad_scores = (probs * (grad_probs - centre) * factor).astype(jnp.bfloat16)
    grad_query = jnp.dot(grad_scores, key_h, preferred_element_type=jnp.float32).astype(jnp.bfloat16)
    grad_key = jnp.dot(grad_scores.T, query_h, preferred_element_type=jnp.float32).astype(jnp.bfloat16)
    grad_value = jnp.dot(probs_low.T, grad_h, preferred_element_type=jnp.float32).astype(jnp.bfloat16)
    return attended, grad_query, grad_key, grad_value


def flatten_heads(stacked):
    return jnp.transpose(stacked, (1, 0, 2)).reshape(stacked.shape[1], -1)


def reference(query, key_in, value, bucket, clip_cost, positions, out_weight, cotangent):
    def one_group(weight_total, index):
        cosine, sine_signed = rotary_tables(positions[:, index, :], HD)
        rot_query = spin(query[index], cosine, sine_signed, 1.0, HD).astype(jnp.bfloat16)
        rot_key = spin(key_in[index], cosine, sine_signed, 1.0, HD).astype(jnp.bfloat16)
        values_here = value[index]
        cot_here = cotangent[index]
        wide = bucket[index]
        rank, order = deal_tables(clip_cost[index], wide)
        clip_row = jnp.where(wide == 1, jnp.zeros((GROUP,), jnp.int32),
                             jnp.arange(GROUP, dtype=jnp.int32) // (GROUP // CLIPS)).astype(jnp.int32)
        grad_dealt = jnp.dot(cot_here, out_weight.T, preferred_element_type=jnp.float32).astype(jnp.bfloat16)
        grad_attended = take_blocks(grad_dealt, rank)

        def per_head(head):
            start = (head * HD).astype(jnp.int32)
            return head_pass(lax.dynamic_slice_in_dim(rot_query, start, HD, 1),
                             lax.dynamic_slice_in_dim(rot_key, start, HD, 1),
                             lax.dynamic_slice_in_dim(values_here, start, HD, 1),
                             lax.dynamic_slice_in_dim(grad_attended, start, HD, 1),
                             clip_row)

        attended, grad_rq, grad_rk, grad_value = lax.map(per_head, jnp.arange(HEADS, dtype=jnp.int32))
        attended = flatten_heads(attended)
        attended_dealt = take_blocks(attended, order)
        mixed = jnp.dot(attended_dealt, out_weight, preferred_element_type=jnp.float32).astype(jnp.bfloat16)
        weight_total = weight_total + jnp.dot(attended_dealt.T, cot_here, preferred_element_type=jnp.float32)
        grad_query = spin(flatten_heads(grad_rq), cosine, sine_signed, -1.0, HD).astype(jnp.bfloat16)
        grad_key = spin(flatten_heads(grad_rk), cosine, sine_signed, -1.0, HD).astype(jnp.bfloat16)
        return weight_total, (mixed, grad_query, grad_key, flatten_heads(grad_value))

    start_total = jnp.zeros((HEADS * HD, D), jnp.float32)
    grad_weight, results = lax.scan(one_group, start_total, jnp.arange(N_DP, dtype=jnp.int32))
    return results[0], results[1], results[2], results[3], grad_weight
```

```python
import functools

import jax
import jax.numpy as jnp
import numpy as np
from jax import lax
from jax.experimental import pallas as pl
from jax.experimental.pallas import tpu as pltpu
from jax.sharding import PartitionSpec as P

MESH = pl.DeviceIdType.MESH
BF = jnp.bfloat16
F32 = jnp.float32

HD = 128
HEADS = 16
CLIPS = 4
ROWS = 128
TOKENS = 2048
SLOT = TOKENS // CLIPS
D = 3072
HALF = D // 2
QB = 256
LOG2E = 1.4426950408889634
FACTOR = HD ** (-0.5)


def rotary_layout(head_dim):
    quarter = head_dim // 4
    rest_span = (head_dim - quarter) // 2
    part_spans = (quarter, rest_span, head_dim - quarter - rest_span)
    partner, signs, axis_of, frequency = [], [], [], []
    offset = 0
    for part_index in range(3):
        part_span = part_spans[part_index]
        half_span = part_span // 2
        for inner_dim in range(part_span):
            pair_index = inner_dim % half_span
            if inner_dim < half_span:
                partner.append(offset + inner_dim + half_span)
                signs.append(-1.0)
            else:
                partner.append(offset + inner_dim - half_span)
                signs.append(1.0)
            axis_of.append(part_index)
            frequency.append(10000.0 ** (-pair_index / half_span))
        offset += part_span
    return np.array(partner), np.array(signs), np.array(axis_of), np.array(frequency)


def partner_matrix():
    partner, signs, _, _ = rotary_layout(HD)
    matrix = np.zeros((HD, HD), np.float32)
    matrix[partner, np.arange(HD)] = signs
    return matrix


def nt(left, right):
    return lax.dot_general(left, right, (((1,), (1,)), ((), ())), preferred_element_type=F32)


def nn(left, right):
    return jnp.dot(left, right, preferred_element_type=F32)


def al(index, size):
    return pl.multiple_of(index, size)


def kernel(
    q_ref, k_ref, v_ref, cos_ref, sin_ref, perm_ref, w_ref, cot_ref, bucket_ref, cost_ref,
    mixed_out, gq_out, gk_out, gv_out, gw_out,
    rq, rk, qh, kh, vh, kt, vt, wbuf, probs, ot, rl, att, dealt, att_tok,
    gd, gdh, dot_t, dq_t, gsend, grecv, cot_t, ct, at_all, gw_send, xr, zs, zr,
    ssem, rsem,
):
    dp, sp = lax.axis_index("dp"), lax.axis_index("sp")
    y, xl, c = dp // 4, (dp // 2) % 2, dp % 2
    z, xh = sp // 2, sp % 2
    x = xh * 2 + xl

    def device(x_, y_, z_, c_):
        return (y_ * 4 + (x_ % 2) * 2 + c_, z_ * 2 + x_ // 2)

    def send(src, dst, s, r, to):
        pltpu.make_async_remote_copy(
            src_ref=src, dst_ref=dst, send_sem=ssem.at[s], recv_sem=rsem.at[r],
            device_id=to, device_id_type=MESH,
        ).start()

    def keep(src, dst, r):
        pltpu.make_async_copy(src, dst, rsem.at[r]).start()

    def wait(view, sem):
        pltpu.make_async_copy(view, view, sem).wait()

    barrier = pltpu.get_barrier_semaphore()

    def greet(to):
        pl.semaphore_signal(barrier, inc=1, device_id=to, device_id_type=MESH)

    @pl.loop(1, 16)
    def _(j):
        greet((dp, lax.rem(sp + j, 16)))

    @pl.loop(1, 8)
    def _(j):
        greet(device(x, (y + j // 2) % 4, z, (c + j) % 2))
        greet(device((x + j // 2) % 4, y, z, (c + j) % 2))

    pl.semaphore_wait(barrier, 29)

    def wblock(half, x_, y_):
        return wbuf.at[half, x_ // 2, :, y_, x_ % 2]

    piece = w_ref.at[pl.ds(al((y * 2 + xl) * 16, 16), 16), pl.ds(al(c * HALF, HALF), HALF)]
    spot = wbuf.at[c, xh, z, y, xl]
    keep(piece, spot, 8)

    @pl.loop(1, 8)
    def _(j):
        send(piece, spot, 8, 8, device(x, y, (z + j) % 8, c))

    cos, sin, perm = cos_ref[...], sin_ref[...], perm_ref[...]

    def turn(block, direction):
        return block.astype(F32) * cos + direction * nn(block, perm) * sin

    mine = pl.ds(al(sp * ROWS, ROWS), ROWS)
    lanes = lambda h: pl.ds(al(h * HD, HD), HD)

    for src, turned, dst, n in ((q_ref, rq, qh, 0), (k_ref, rk, kh, 1)):
        turned[sp] = turn(src[:, lanes(sp)], 1.0).astype(BF)
        keep(turned.at[sp], dst.at[mine], n)

        @pl.loop(1, 16)
        def _(j, src=src, turned=turned, dst=dst, n=n):
            h = lax.rem(sp + j, 16)
            turned[h] = turn(src[:, lanes(h)], 1.0).astype(BF)
            send(turned.at[h], dst.at[mine], n, n, (dp, h))

    keep(v_ref.at[:, lanes(sp)], vh.at[mine], 2)

    @pl.loop(1, 16)
    def _(j):
        h = lax.rem(sp + j, 16)
        send(v_ref.at[:, lanes(h)], vh.at[mine], 2, 2, (dp, h))

    def ring2(j):
        return (x + c * j) % 4, (y + (1 - c) * j) % 4

    def ring3(j):
        return (x + (1 - c) * j) % 4, (y + c * j) % 4

    def pass_on(i, x_, y_):
        block = wblock(c, x_, y_)
        send(block, block, 13, 13, device(x, y, z, 1 - c))
        for j in range(1, 4):
            tx, ty = ring3(j)
            send(block, block, 14, 17 + i * 3 + j - 1, device(tx, ty, z, c))

    own = wblock(c, x, y)
    wait(own, rsem.at[8])
    for j in range(1, 4):
        tx, ty = ring2(j)
        send(own, own, 9, 13 + j, device(tx, ty, z, c))
    pass_on(0, x, y)
    for j in range(1, 4):
        bx, by = ring2(4 - j)
        wait(wblock(c, bx, by), rsem.at[13 + j])
        pass_on(j, bx, by)

    wait(qh, rsem.at[0])
    wait(kh, rsem.at[1])
    wait(vh, rsem.at[2])
    kt[...] = kh[...].T
    vt[...] = vh[...].T
    narrow = jnp.where(bucket_ref[0] == 1, 0.0, -1e30).astype(F32)

    @pl.loop(0, TOKENS // QB)
    def _(b):
        cols = pl.ds(al(b * QB, QB), QB)
        slot = b // (SLOT // QB)
        scores = nt(kh[...], qh[cols, :]) * (FACTOR * LOG2E)
        parts = [
            scores[i * SLOT : (i + 1) * SLOT] + jnp.where(slot == i, 0.0, narrow)
            for i in range(CLIPS)
        ]
        scores = jnp.concatenate(parts, axis=0)
        top = jnp.max(scores, axis=0, keepdims=True)
        low = jnp.exp2(scores - top).astype(BF)
        probs[:, cols] = low
        scale = 1.0 / jnp.sum(low.astype(F32), axis=0, keepdims=True)
        rl[:, cols] = scale
        out = nn(vt[...], low) * scale
        ot[:, cols] = out
        att[cols, :] = out.T.astype(BF)

    costs = [cost_ref[0, k] for k in range(CLIPS)]
    wide = bucket_ref[0] == 1
    rank = []
    for k in range(CLIPS):
        count = jnp.int32(0)
        for j in range(CLIPS):
            if j != k:
                above = costs[j] >= costs[k] if j < k else costs[j] > costs[k]
                count = count + jnp.where(above, 1, 0)
        rank.append(jnp.where(wide, k, count))
    choose = [[jnp.where(rank[k] == r, 1.0, 0.0).astype(F32) for k in range(CLIPS)] for r in range(CLIPS)]

    slots = [att[k * SLOT : (k + 1) * SLOT, :].astype(F32) for k in range(CLIPS)]
    for r in range(CLIPS):
        picked = sum(slots[k] * choose[r][k] for k in range(CLIPS))
        dealt[r * SLOT : (r + 1) * SLOT, :] = picked.astype(BF)

    here = att_tok.at[xh, :, lanes(z)]
    keep(dealt.at[mine], here, 3)

    @pl.loop(1, 16)
    def _(j):
        t = lax.rem(sp + j, 16)
        send(dealt.at[pl.ds(al(t * ROWS, ROWS), ROWS)], here, 3, 3, (dp, t))

    for i in range(D // 128):
        cot_t[i * 128 : (i + 1) * 128, :] = cot_ref[:, i * 128 : (i + 1) * 128].T
    me8 = y * 2 + c
    ct_here = ct.at[:, lanes(me8)]
    keep(cot_t.at[pl.ds(al(y * 768, 768), 768)], ct_here, 10)

    @pl.loop(1, 8)
    def _(j):
        ty, tc = (y + j // 2) % 4, (c + j) % 2
        send(cot_t.at[pl.ds(al(ty * 768, 768), 768)], ct_here, 10, 10, device(x, ty, z, tc))

    for i in range(4):
        for j in range(1, 4):
            bx, by = ring2(4 - i) if i else (x, y)
            bx, by = (bx + (1 - c) * (4 - j)) % 4, (by + c * (4 - j)) % 4
            block = wblock(c, bx, by)
            wait(block, rsem.at[17 + i * 3 + j - 1])
            send(block, block, 13, 13, device(x, y, z, 1 - c))
    wait(wbuf.at[1 - c], rsem.at[13])

    def grad_of(h):
        first = wbuf[0, h % 2, h // 2].reshape(HD, HALF)
        second = wbuf[1, h % 2, h // 2].reshape(HD, HALF)
        gd[h] = (nt(cot_ref[:, :HALF], first) + nt(cot_ref[:, HALF:], second)).astype(BF)

    grad_of(sp)
    keep(gd.at[sp], gdh.at[mine], 4)

    @pl.loop(1, 16)
    def _(j):
        h = lax.rem(sp + j, 16)
        grad_of(h)
        send(gd.at[h], gdh.at[mine], 4, 4, (dp, h))

    wait(att_tok, rsem.at[3])
    at_here = at_all.at[pl.ds(al(me8 * ROWS, ROWS), ROWS)]
    keep(att_tok.at[c], at_here, 11)

    @pl.loop(1, 8)
    def _(j):
        ty, tc = (y + j // 2) % 4, (c + j) % 2
        send(att_tok.at[tc], at_here, 11, 11, device(x, ty, z, tc))

    for half in range(2):

        @pl.loop(0, HALF // 512)
        def _(i, half=half):
            cols = pl.ds(al(i * 512, 512), 512)
            total = nn(att_tok[0], wbuf[half, 0, :, :, :, :, cols].reshape(1024, 512))
            total += nn(att_tok[1], wbuf[half, 1, :, :, :, :, cols].reshape(1024, 512))
            mixed_out[:, pl.ds(al(half * HALF + i * 512, 512), 512)] = total.astype(BF)

    wait(gdh, rsem.at[4])
    slots = [gdh[k * SLOT : (k + 1) * SLOT, :].astype(F32) for k in range(CLIPS)]
    for k in range(CLIPS):
        picked = sum(slots[r] * choose[r][k] for r in range(CLIPS))
        dot_t[:, k * SLOT : (k + 1) * SLOT] = picked.T.astype(BF)

    def give(n, t):
        @pl.when(t == sp)
        def _():
            keep(gsend.at[n, t], grecv.at[n, sp], 5 + n)

        @pl.when(t != sp)
        def _():
            send(gsend.at[n, t], grecv.at[n, sp], 5 + n, 5 + n, (dp, t))

    scale = rl[...]
    scaled = (dot_t[...].astype(F32) * scale).astype(BF)
    centre = jnp.sum(dot_t[...].astype(F32) * ot[...], axis=0, keepdims=True)

    @pl.loop(0, TOKENS // QB)
    def _(i):
        b = (i + sp // 2) % (TOKENS // QB)
        rows = pl.ds(al(b * QB, QB), QB)
        low = probs[rows, :]
        value_grad = nt(low, scaled).astype(BF)
        gsend[0, b * 2] = value_grad[:ROWS]
        gsend[0, b * 2 + 1] = value_grad[ROWS:]
        give(0, b * 2)
        give(0, b * 2 + 1)

    scale = scale * FACTOR
    centre = centre * scale
    dq_t[...] = jnp.zeros_like(dq_t)

    @pl.loop(0, TOKENS // QB)
    def _(i):
        b = (i + sp // 2) % (TOKENS // QB)
        rows = pl.ds(al(b * QB, QB), QB)
        grad_probs = nn(vh[rows, :], dot_t[...])
        grad_scores = (probs[rows, :].astype(F32) * (grad_probs * scale - centre)).astype(BF)
        key_grad = nn(grad_scores, qh[...]).astype(BF)
        gsend[1, b * 2] = key_grad[:ROWS]
        gsend[1, b * 2 + 1] = key_grad[ROWS:]
        give(1, b * 2)
        give(1, b * 2 + 1)
        dq_t[...] += nn(kt[:, rows], grad_scores)

    @pl.loop(0, HEADS)
    def _(i):
        t = lax.rem(sp + i, 16)
        gsend[2, t] = dq_t[:, lanes(t)].T.astype(BF)
        give(2, t)

    wait(ct, rsem.at[10])
    wait(at_all, rsem.at[11])
    for b in range(4):
        gw_send[b] = nn(ct[b * 192 : (b + 1) * 192, :], at_all[...]).astype(BF)
        tx, tc = 2 * c + b // 2, b % 2
        same = jnp.logical_and(tx == x, tc == c)

        @pl.when(same)
        def _(b=b):
            keep(gw_send.at[b], xr.at[x], 12)

        @pl.when(jnp.logical_not(same))
        def _(b=b, tx=tx, tc=tc):
            send(gw_send.at[b], xr.at[x], 12, 12, device(tx, y, z, tc))

    wait(xr, rsem.at[12])
    for i in range(8):
        cols = slice(i * HD, (i + 1) * HD)
        total = sum(xr[j, :, cols].astype(F32) for j in range(4))
        zs[i] = total.astype(BF)
    keep(zs.at[z], zr.at[z], 9)

    @pl.loop(1, 8)
    def _(j):
        tz = (z + j) % 8
        send(zs.at[tz], zr.at[z], 15, 9, device(x, y, tz, c))

    wait(grecv.at[0], rsem.at[5])
    for h in range(HEADS):
        gv_out[:, h * HD : (h + 1) * HD] = grecv[0, h]

    for n, out in ((1, gk_out), (2, gq_out)):
        wait(grecv.at[n], rsem.at[5 + n])

        @pl.loop(0, HEADS)
        def _(h, n=n, out=out):
            out[:, lanes(h)] = turn(grecv[n, h], -1.0).astype(BF)

    wait(zr, rsem.at[9])
    gw_out[...] = sum(zr[i].astype(F32) for i in range(8))

    most = lambda ref: ref.at[pl.ds(0, 15)]
    wait(most(rq), ssem.at[0])
    wait(most(rk), ssem.at[1])
    wait(most(rk), ssem.at[2])
    wait(most(gd), ssem.at[3])
    wait(most(gd), ssem.at[4])
    for n in range(3):
        wait(most(gsend.at[n]), ssem.at[5 + n])
    wait(wbuf.at[0, 0, pl.ds(0, 7), 0, 0], ssem.at[8])
    wait(wbuf.at[c], ssem.at[13])
    wait(wbuf.at[0, 0, :, pl.ds(0, 3), 0], ssem.at[9])
    wait(wbuf.at[0, :, :, pl.ds(0, 3), :], ssem.at[14])
    wait(zs.at[pl.ds(0, 7)], ssem.at[15])
    wait(ct.at[:, pl.ds(0, 7 * HD)], ssem.at[10])
    wait(at_all.at[pl.ds(0, 7 * ROWS)], ssem.at[11])
    wait(gw_send.at[pl.ds(0, 3)], ssem.at[12])

    @pl.when(c != xh)
    def _():
        wait(gw_send.at[0], ssem.at[12])


def local(query, key_in, value, bucket, clip_cost, positions, out_weight, cotangent):
    _, _, axis_of, frequency = rotary_layout(HD)
    angles = jnp.transpose(positions[:, 0, :].astype(F32))
    angles = jnp.concatenate(
        [jnp.broadcast_to(angles[:, a : a + 1], (ROWS, int(np.sum(axis_of == a)))) for a in range(3)], axis=1
    ) * jnp.asarray(frequency, F32)
    perm = jnp.asarray(partner_matrix(), BF)

    vmem = pl.BlockSpec(memory_space=pltpu.VMEM)
    smem = pl.BlockSpec(memory_space=pltpu.SMEM)
    bf = lambda *shape: pltpu.VMEM(shape, BF)
    f32 = lambda *shape: pltpu.VMEM(shape, F32)
    shape = jax.ShapeDtypeStruct
    mixed, grad_query, grad_key, grad_value, grad_weight = pl.pallas_call(
        kernel,
        out_shape=(
            shape((ROWS, D), BF),
            shape((ROWS, TOKENS), BF),
            shape((ROWS, TOKENS), BF),
            shape((ROWS, TOKENS), BF),
            shape((192, HD), F32),
        ),
        in_specs=[vmem] * 8 + [smem] * 2,
        out_specs=(vmem,) * 5,
        scratch_shapes=[
            bf(16, ROWS, HD), bf(16, ROWS, HD),
            bf(TOKENS, HD), bf(TOKENS, HD), bf(TOKENS, HD),
            bf(HD, TOKENS), bf(HD, TOKENS),
            bf(2, 2, 8, 4, 2, 16, HALF),
            bf(TOKENS, TOKENS),
            f32(HD, TOKENS), f32(1, TOKENS),
            bf(TOKENS, HD), bf(TOKENS, HD),
            bf(2, ROWS, 1024),
            bf(16, ROWS, HD), bf(TOKENS, HD),
            bf(HD, TOKENS), f32(HD, TOKENS),
            bf(3, 16, ROWS, HD), bf(3, 16, ROWS, HD),
            bf(D, ROWS), bf(768, 1024), bf(1024, 1024),
            bf(4, 192, 1024), bf(4, 192, 1024),
            bf(8, 192, HD), bf(8, 192, HD),
            pltpu.SemaphoreType.DMA((16,)), pltpu.SemaphoreType.DMA((32,)),
        ],
        compiler_params=pltpu.CompilerParams(
            collective_id=0, has_side_effects=True, vmem_limit_bytes=62 * 2**20
        ),
    )(
        query[0], key_in[0], value[0], jnp.cos(angles), jnp.sin(angles), perm,
        out_weight, cotangent[0], bucket, clip_cost,
    )
    return mixed[None], grad_query[None], grad_key[None], grad_value[None], grad_weight.T


def solution(mesh):
    in_specs = (
        P("dp", "sp", None),
        P("dp", "sp", None),
        P("dp", "sp", None),
        P("dp"),
        P("dp", None),
        P(None, "dp", "sp"),
        P("sp", None),
        P("dp", "sp", None),
    )
    out_specs = (
        P("dp", "sp", None),
        P("dp", "sp", None),
        P("dp", "sp", None),
        P("dp", "sp", None),
        P("sp", "dp"),
    )
    return jax.shard_map(local, mesh=mesh, in_specs=in_specs, out_specs=out_specs, check_vma=False)
```

```python
import functools

import jax
import jax.numpy as jnp
import numpy as np
from jax import lax
from jax.experimental import pallas as pl
from jax.experimental.pallas import tpu as pltpu
from jax.sharding import PartitionSpec as P

MESH = pl.DeviceIdType.MESH
BF = jnp.bfloat16
F32 = jnp.float32

HD = 128
HEADS = 16
CLIPS = 4
ROWS = 128
TOKENS = 2048
SLOT = TOKENS // CLIPS
D = 3072
PARTS = 2
SPLIT = 1
WIDE = D // PARTS
QB = 256
LOG2E = 1.4426950408889634
FACTOR = HD ** (-0.5)


def rotary_layout(head_dim):
    quarter = head_dim // 4
    rest_span = (head_dim - quarter) // 2
    part_spans = (quarter, rest_span, head_dim - quarter - rest_span)
    partner, signs, axis_of, frequency = [], [], [], []
    offset = 0
    for part_index in range(3):
        part_span = part_spans[part_index]
        half_span = part_span // 2
        for inner_dim in range(part_span):
            pair_index = inner_dim % half_span
            if inner_dim < half_span:
                partner.append(offset + inner_dim + half_span)
                signs.append(-1.0)
            else:
                partner.append(offset + inner_dim - half_span)
                signs.append(1.0)
            axis_of.append(part_index)
            frequency.append(10000.0 ** (-pair_index / half_span))
        offset += part_span
    return np.array(partner), np.array(signs), np.array(axis_of), np.array(frequency)


def partner_matrix():
    partner, signs, _, _ = rotary_layout(HD)
    matrix = np.zeros((HD, HD), np.float32)
    matrix[partner, np.arange(HD)] = signs
    return matrix


def nt(left, right):
    return lax.dot_general(left, right, (((1,), (1,)), ((), ())), preferred_element_type=F32)


def nn(left, right):
    return jnp.dot(left, right, preferred_element_type=F32)


def al(index, size):
    return pl.multiple_of(index, size)


def kernel(
    q_ref, k_ref, v_ref, cos_ref, sin_ref, perm_ref, w_ref, cot_ref, bucket_ref, cost_ref,
    mixed_out, gq_out, gk_out, gv_out, gw_out,
    rin, rel, qh, kh, vh, kt, vt, wbuf, probs, ot, rl, att, dealt, att_tok,
    gd, gdh, dot_t, dq_t, gsend, grecv, cot_t, ct, at_all, gw_send, xr, zs, zr,
    ssem, rsem,
):
    dp, sp = lax.axis_index("dp"), lax.axis_index("sp")
    y, xl, c = dp // 4, (dp // 2) % 2, dp % 2
    z, xh = sp // 2, sp % 2
    x = xh * 2 + xl

    def device(x_, y_, z_, c_):
        return (y_ * 4 + (x_ % 2) * 2 + c_, z_ * 2 + x_ // 2)

    def send(src, dst, s, r, to):
        pltpu.make_async_remote_copy(
            src_ref=src, dst_ref=dst, send_sem=ssem.at[s], recv_sem=rsem.at[r],
            device_id=to, device_id_type=MESH,
        ).start()

    def keep(src, dst, r):
        pltpu.make_async_copy(src, dst, rsem.at[r]).start()

    def wait(view, sem):
        pltpu.make_async_copy(view, view, sem).wait()

    barrier = pltpu.get_barrier_semaphore()

    def greet(to):
        pl.semaphore_signal(barrier, inc=1, device_id=to, device_id_type=MESH)

    @pl.loop(1, 16)
    def _(j):
        greet((dp, lax.rem(sp + j, 16)))

    @pl.loop(1, 8)
    def _(j):
        greet(device(x, (y + j // 2) % 4, z, (c + j) % 2))
        greet(device((x + j // 2) % 4, y, z, (c + j) % 2))

    pl.semaphore_wait(barrier, 29)

    def per_core(run):
        @pl.when(c == 0)
        def _():
            run(0, pl.ds(0, SPLIT))

        @pl.when(c == 1)
        def _():
            run(1, pl.ds(SPLIT, PARTS - SPLIT))

    def give_piece(core, parts):
        for t in range(parts.start, parts.start + parts.size):
            piece = w_ref.at[pl.ds(al((y * 2 + xl) * 16, 16), 16), pl.ds(t * WIDE, WIDE)]
            spot = wbuf.at[t, xh, z, y, xl]
            keep(piece, spot, 8)

            @pl.loop(1, 8)
            def _(j, piece=piece, spot=spot):
                send(piece, spot, 8, 8, device(x, y, (z + j) % 8, c))

    per_core(give_piece)

    lanes = lambda h: pl.ds(al(h * HD, HD), HD)
    sibling = device(x, y, z, 1 - c)
    me8 = y * 2 + c
    for i in range(D // 128):
        cot_t[i * 128 : (i + 1) * 128, :] = cot_ref[:, i * 128 : (i + 1) * 128].T
    quarter = cot_t.at[pl.ds(al(y * 768, 768), 768)]
    keep(quarter, ct.at[:, lanes(me8)], 10)
    send(quarter, ct.at[:, lanes(me8)], 10, 10, sibling)
    for j in range(1, 4):
        ty = (y + j) % 4
        send(cot_t.at[pl.ds(al(ty * 768, 768), 768)], ct.at[:, lanes(me8)], 10, 36 + j, device(x, ty, z, c))

    def hand_over_cotangent():
        for j in range(1, 4):
            view = ct.at[:, lanes((y + 4 - j) % 4 * 2 + c)]
            wait(view, rsem.at[36 + j])
            send(view, view, 19, 10, sibling)

    cos, sin, perm = cos_ref[...], sin_ref[...], perm_ref[...]

    def turn(block, direction):
        return block.astype(F32) * cos + direction * nn(block, perm) * sin

    mine = pl.ds(al(sp * ROWS, ROWS), ROWS)

    partner = (dp, z * 2 + 1 - xh)
    theirs = pl.ds(al(partner[1] * ROWS, ROWS), ROWS)

    def fill(n, src, side):
        @pl.loop(0, 8)
        def _(i):
            part = src[:, lanes(i * 2 + side)]
            rin[n, side, i] = part if n == 2 else turn(part, 1.0).astype(BF)

    def cross(n):
        send(rin.at[n, 1 - xh], rel.at[n], 21 + n, 44 + n, partner)

    def along(n, view, dst, rows, s):
        keep(view.at[z], dst.at[rows], n)

        @pl.loop(1, 8)
        def _(j):
            tz = lax.rem(z + j, 8)
            send(view.at[tz], dst.at[rows], s, n, (dp, tz * 2 + xh))

    arrays = ((0, q_ref, qh), (1, k_ref, kh), (2, v_ref, vh))

    def hand_on(n, dst):
        wait(rel.at[n], rsem.at[44 + n])
        along(n, rel.at[n], dst, theirs, 24 + n)

    for n, src, _ in arrays[:2]:
        fill(n, src, 1 - xh)
        cross(n)
    for n, src, _ in arrays:
        fill(n, src, xh)
    fill(2, v_ref, 1 - xh)

    def at(core, i, k):
        return ((x + 8 + i) % 4, (y + 8 + k) % 4) if core else ((x + 8 + k) % 4, (y + 8 + i) % 4)

    def block(core, parts, i, k):
        bx, by = at(core, i, k)
        return wbuf.at[parts, bx // 2, :, by, bx % 2]

    def half_of(core, parts, i, k, m):
        bx, by = at(core, i, k)
        return wbuf.at[parts, bx // 2, pl.ds(4 * m, 4), by, bx % 2]

    def ring_to(core, i, k):
        return device(*at(core, i, k), z, c)

    order = (0, -1, 1, 2)

    def share(core, parts, n):
        view = block(core, parts, order[n], 0)
        send(view, view, 14, 21 + 4 * n, ring_to(core, 0, 1))
        send(view, view, 14, 22 + 4 * n, ring_to(core, 0, -1))
        send(view, view, 13, 13, sibling)

    def pass_on(n):
        def run(core, parts):
            for side, m in ((-1, 0), (1, 1)):
                view = block(core, parts, order[n], side)
                part = half_of(core, parts, order[n], side, m)
                wait(view, rsem.at[21 + 4 * n + m])
                send(part, part, 15, 23 + 4 * n + m, ring_to(core, 0, -side))
                send(view, view, 13, 13, sibling)

        per_core(run)

    def first_ring_start(core, parts):
        own = block(core, parts, 0, 0)
        wait(own, rsem.at[8])
        send(own, own, 9, 17, ring_to(core, 1, 0))
        send(own, own, 9, 18, ring_to(core, -1, 0))
        share(core, parts, 0)

    def first_ring(core, parts):
        for n, side, m in ((1, -1, 0), (2, 1, 1)):
            part = half_of(core, parts, side, 0, m)
            wait(block(core, parts, side, 0), rsem.at[17 + m])
            send(part, part, 16, 19 + m, ring_to(core, -side, 0))
            share(core, parts, n)

    def first_ring_end(core, parts):
        for m in range(2):
            wait(half_of(core, parts, 2, 0, m), rsem.at[19 + m])
        share(core, parts, 3)

    def second_ring_end(core, parts):
        for n in range(4):
            for m in range(2):
                wait(half_of(core, parts, order[n], 2, m), rsem.at[23 + 4 * n + m])
            view = block(core, parts, order[n], 2)
            send(view, view, 13, 13, sibling)

    def others_come(core, parts):
        rest = pl.ds(0, SPLIT) if core else pl.ds(SPLIT, PARTS - SPLIT)
        wait(wbuf.at[rest], rsem.at[13])

    per_core(first_ring_start)
    for n, _, dst in arrays[:2]:
        along(n, rin.at[n, xh], dst, mine, n)
    for n, _, dst in arrays[:2]:
        hand_on(n, dst)
    along(2, rin.at[2, xh], vh, mine, 2)
    per_core(first_ring)
    cross(2)
    hand_over_cotangent()
    pass_on(0)
    per_core(first_ring_end)
    hand_on(2, vh)
    pass_on(1)

    wait(qh, rsem.at[0])
    wait(kh, rsem.at[1])
    narrow = jnp.where(bucket_ref[0] == 1, 0.0, -1e30).astype(F32)

    def weigh(b):
        cols = pl.ds(al(b * QB, QB), QB)
        slot = b // (SLOT // QB)
        scores = nt(kh[...], qh[cols, :]) * (FACTOR * LOG2E)
        parts = [
            scores[i * SLOT : (i + 1) * SLOT] + jnp.where(slot == i, 0.0, narrow)
            for i in range(CLIPS)
        ]
        scores = jnp.concatenate(parts, axis=0)
        top = jnp.max(scores, axis=0, keepdims=True)
        low = jnp.exp2(scores - top).astype(BF)
        probs[:, cols] = low
        scale = 1.0 / jnp.sum(low.astype(F32), axis=0, keepdims=True)
        rl[:, cols] = scale

    pl.loop(0, 4)(weigh)
    pass_on(2)
    pl.loop(4, TOKENS // QB)(weigh)
    pass_on(3)

    wait(vh, rsem.at[2])
    vt[...] = vh[...].T

    @pl.loop(0, TOKENS // QB)
    def _(b):
        cols = pl.ds(al(b * QB, QB), QB)
        out = nn(vt[...], probs[:, cols]) * rl[:, cols]
        ot[:, cols] = out
        att[cols, :] = out.T.astype(BF)

    costs = [cost_ref[0, k] for k in range(CLIPS)]
    wide = bucket_ref[0] == 1
    rank = []
    for k in range(CLIPS):
        count = jnp.int32(0)
        for j in range(CLIPS):
            if j != k:
                above = costs[j] >= costs[k] if j < k else costs[j] > costs[k]
                count = count + jnp.where(above, 1, 0)
        rank.append(jnp.where(wide, k, count))
    choose = [[jnp.where(rank[k] == r, 1.0, 0.0).astype(F32) for k in range(CLIPS)] for r in range(CLIPS)]

    slots = [att[k * SLOT : (k + 1) * SLOT, :].astype(F32) for k in range(CLIPS)]
    for r in range(CLIPS):
        picked = sum(slots[k] * choose[r][k] for k in range(CLIPS))
        dealt[r * SLOT : (r + 1) * SLOT, :] = picked.astype(BF)

    here = att_tok.at[xh, :, lanes(z)]
    keep(dealt.at[mine], here, 3)

    @pl.loop(1, 16)
    def _(j):
        t = lax.rem(sp + j, 16)
        send(dealt.at[pl.ds(al(t * ROWS, ROWS), ROWS)], here, 3, 3, (dp, t))

    per_core(second_ring_end)

    per_core(others_come)

    def grad_of(h):
        total = sum(
            nt(cot_ref[:, t * WIDE : (t + 1) * WIDE], wbuf[t, h % 2, h // 2].reshape(HD, WIDE))
            for t in range(PARTS)
        )
        gd[h] = total.astype(BF)

    grad_of(sp)
    keep(gd.at[sp], gdh.at[mine], 4)

    @pl.loop(1, 16)
    def _(j):
        h = lax.rem(sp + j, 16)
        grad_of(h)
        send(gd.at[h], gdh.at[mine], 4, 4, (dp, h))

    wait(att_tok, rsem.at[3])
    def rows_of(ty, tc, first=0, count=ROWS):
        return at_all.at[pl.ds(al((ty * 2 + tc) * ROWS + first, count), count)]

    at_here = rows_of(y, c)
    keep(att_tok.at[c], at_here, 11)
    for tc in range(2):
        send(att_tok.at[tc], at_here, 11, 40 + c, device(x, (y + 1) % 4, z, tc))
        send(att_tok.at[tc], at_here, 11, 42 + c, device(x, (y + 3) % 4, z, tc))
    send(att_tok.at[1 - c], at_here, 11, 11, sibling)

    for t in range(PARTS):

        @pl.loop(0, WIDE // 512)
        def _(i, t=t):
            cols = pl.ds(al(i * 512, 512), 512)
            total = nn(att_tok[0], wbuf[t, 0, :, :, :, :, cols].reshape(1024, 512))
            total += nn(att_tok[1], wbuf[t, 1, :, :, :, :, cols].reshape(1024, 512))
            mixed_out[:, pl.ds(al(t * WIDE + i * 512, 512), 512)] = total.astype(BF)

    for m, step in ((0, 3), (1, 1)):
        ty = (y + step) % 4
        for tc in range(2):
            wait(rows_of(ty, tc), rsem.at[40 + 2 * m + tc])
            part = rows_of(ty, tc, 64 * m, 64)
            send(part, part, 18, 11, device(x, (y + 4 - step) % 4, z, c))

    kt[...] = kh[...].T

    wait(gdh, rsem.at[4])
    slots = [gdh[k * SLOT : (k + 1) * SLOT, :].astype(F32) for k in range(CLIPS)]
    for k in range(CLIPS):
        picked = sum(slots[r] * choose[r][k] for r in range(CLIPS))
        dot_t[:, k * SLOT : (k + 1) * SLOT] = picked.T.astype(BF)

    def give(n, t):
        @pl.when(t == sp)
        def _():
            keep(gsend.at[n, t], grecv.at[n, sp], 5 + n)

        @pl.when(t != sp)
        def _():
            send(gsend.at[n, t], grecv.at[n, sp], 5 + n, 5 + n, (dp, t))

    scale = rl[...]
    scaled = (dot_t[...].astype(F32) * scale).astype(BF)
    centre = jnp.sum(dot_t[...].astype(F32) * ot[...], axis=0, keepdims=True)

    @pl.loop(0, TOKENS // QB)
    def _(i):
        b = (i + sp // 2) % (TOKENS // QB)
        rows = pl.ds(al(b * QB, QB), QB)
        low = probs[rows, :]
        value_grad = nt(low, scaled).astype(BF)
        gsend[0, b * 2] = value_grad[:ROWS]
        gsend[0, b * 2 + 1] = value_grad[ROWS:]
        give(0, b * 2)
        give(0, b * 2 + 1)

    wait(ct.at[:, pl.ds(0, 5 * HD)], rsem.at[10])
    wait(at_all.at[pl.ds(0, 4 * ROWS)], rsem.at[11])
    for b in range(4):
        gw_send[b] = nn(ct[b * 192 : (b + 1) * 192, :], at_all[...]).astype(BF)
        tx, tc = 2 * c + b // 2, b % 2
        same = jnp.logical_and(tx == x, tc == c)

        @pl.when(same)
        def _(b=b):
            keep(gw_send.at[b], xr.at[x], 12)

        @pl.when(jnp.logical_not(same))
        def _(b=b, tx=tx, tc=tc):
            send(gw_send.at[b], xr.at[x], 12, 12, device(tx, y, z, tc))

    scale = scale * FACTOR
    centre = centre * scale
    dq_t[...] = jnp.zeros_like(dq_t)

    @pl.loop(0, TOKENS // QB)
    def _(i):
        b = (i + sp // 2) % (TOKENS // QB)
        rows = pl.ds(al(b * QB, QB), QB)
        grad_probs = nn(vh[rows, :], dot_t[...])
        grad_scores = (probs[rows, :].astype(F32) * (grad_probs * scale - centre)).astype(BF)
        key_grad = nn(grad_scores, qh[...]).astype(BF)
        gsend[1, b * 2] = key_grad[:ROWS]
        gsend[1, b * 2 + 1] = key_grad[ROWS:]
        give(1, b * 2)
        give(1, b * 2 + 1)
        dq_t[...] += nn(kt[:, rows], grad_scores)

    @pl.loop(0, HEADS)
    def _(i):
        t = lax.rem(sp + i, 16)
        gsend[2, t] = dq_t[:, lanes(t)].T.astype(BF)
        give(2, t)

    wait(xr, rsem.at[12])
    for i in range(8):
        cols = slice(i * HD, (i + 1) * HD)
        total = sum(xr[j, :, cols].astype(F32) for j in range(4))
        zs[i] = total.astype(BF)
    keep(zs.at[z], zr.at[z], 9)

    @pl.loop(1, 8)
    def _(j):
        tz = (z + j) % 8
        send(zs.at[tz], zr.at[z], 17, 9, device(x, y, tz, c))

    wait(grecv.at[0], rsem.at[5])
    for h in range(HEADS):
        gv_out[:, h * HD : (h + 1) * HD] = grecv[0, h]

    for n, out in ((1, gk_out), (2, gq_out)):
        wait(grecv.at[n], rsem.at[5 + n])

        @pl.loop(0, HEADS)
        def _(h, n=n, out=out):
            out[:, lanes(h)] = turn(grecv[n, h], -1.0).astype(BF)

    wait(zr, rsem.at[9])
    gw_out[...] = sum(zr[i].astype(F32) for i in range(8))

    most = lambda ref: ref.at[pl.ds(0, 15)]
    for n in range(3):
        wait(rel.at[n, pl.ds(0, 7)], ssem.at[n])
        wait(rel.at[n], ssem.at[21 + n])
        wait(rel.at[n, pl.ds(0, 7)], ssem.at[24 + n])
    wait(most(gd), ssem.at[3])
    wait(most(gd), ssem.at[4])
    for n in range(3):
        wait(most(gsend.at[n]), ssem.at[5 + n])

    def weights_left(core, parts):
        wait(wbuf.at[parts, 0, pl.ds(0, 7), 0, 0], ssem.at[8])
        wait(wbuf.at[parts], ssem.at[13])
        wait(wbuf.at[parts, 0, :, 0, :], ssem.at[9])
        wait(wbuf.at[parts, 0, :, 0, 0], ssem.at[16])
        wait(wbuf.at[parts, 0], ssem.at[14])
        wait(wbuf.at[parts, 0, :, :, 0], ssem.at[15])

    per_core(weights_left)
    wait(zs.at[pl.ds(0, 7)], ssem.at[17])
    wait(ct.at[:, pl.ds(0, 4 * HD)], ssem.at[10])
    wait(ct.at[:, pl.ds(0, 3 * HD)], ssem.at[19])
    wait(at_all.at[pl.ds(0, 5 * ROWS)], ssem.at[11])
    wait(at_all.at[pl.ds(0, 2 * ROWS)], ssem.at[18])
    wait(gw_send.at[pl.ds(0, 3)], ssem.at[12])

    @pl.when(c != xh)
    def _():
        wait(gw_send.at[0], ssem.at[12])


def local(query, key_in, value, bucket, clip_cost, positions, out_weight, cotangent):
    _, _, axis_of, frequency = rotary_layout(HD)
    angles = jnp.transpose(positions[:, 0, :].astype(F32))
    angles = jnp.concatenate(
        [jnp.broadcast_to(angles[:, a : a + 1], (ROWS, int(np.sum(axis_of == a)))) for a in range(3)], axis=1
    ) * jnp.asarray(frequency, F32)
    perm = jnp.asarray(partner_matrix(), BF)

    vmem = pl.BlockSpec(memory_space=pltpu.VMEM)
    smem = pl.BlockSpec(memory_space=pltpu.SMEM)
    bf = lambda *shape: pltpu.VMEM(shape, BF)
    f32 = lambda *shape: pltpu.VMEM(shape, F32)
    shape = jax.ShapeDtypeStruct
    mixed, grad_query, grad_key, grad_value, grad_weight = pl.pallas_call(
        kernel,
        out_shape=(
            shape((ROWS, D), BF),
            shape((ROWS, TOKENS), BF),
            shape((ROWS, TOKENS), BF),
            shape((ROWS, TOKENS), BF),
            shape((192, HD), F32),
        ),
        in_specs=[vmem] * 8 + [smem] * 2,
        out_specs=(vmem,) * 5,
        scratch_shapes=[
            bf(3, 2, 8, ROWS, HD), bf(3, 8, ROWS, HD),
            bf(TOKENS, HD), bf(TOKENS, HD), bf(TOKENS, HD),
            bf(HD, TOKENS), bf(HD, TOKENS),
            bf(PARTS, 2, 8, 4, 2, 16, WIDE),
            bf(TOKENS, TOKENS),
            f32(HD, TOKENS), f32(1, TOKENS),
            bf(TOKENS, HD), bf(TOKENS, HD),
            bf(2, ROWS, 1024),
            bf(16, ROWS, HD), bf(TOKENS, HD),
            bf(HD, TOKENS), f32(HD, TOKENS),
            bf(3, 16, ROWS, HD), bf(3, 16, ROWS, HD),
            bf(D, ROWS), bf(768, 1024), bf(1024, 1024),
            bf(4, 192, 1024), bf(4, 192, 1024),
            bf(8, 192, HD), bf(8, 192, HD),
            pltpu.SemaphoreType.DMA((27,)), pltpu.SemaphoreType.DMA((47,)),
        ],
        compiler_params=pltpu.CompilerParams(
            collective_id=0, has_side_effects=True, vmem_limit_bytes=62 * 2**20
        ),
    )(
        query[0], key_in[0], value[0], jnp.cos(angles), jnp.sin(angles), perm,
        out_weight, cotangent[0], bucket, clip_cost,
    )
    return mixed[None], grad_query[None], grad_key[None], grad_value[None], grad_weight.T


def solution(mesh):
    in_specs = (
        P("dp", "sp", None),
        P("dp", "sp", None),
        P("dp", "sp", None),
        P("dp"),
        P("dp", None),
        P(None, "dp", "sp"),
        P("sp", None),
        P("dp", "sp", None),
    )
    out_specs = (
        P("dp", "sp", None),
        P("dp", "sp", None),
        P("dp", "sp", None),
        P("dp", "sp", None),
        P("sp", "dp"),
    )
    return jax.shard_map(local, mesh=mesh, in_specs=in_specs, out_specs=out_specs, check_vma=False)
```

```python
import functools

import jax
import jax.numpy as jnp
import numpy as np
from jax import lax
from jax.experimental import pallas as pl
from jax.experimental.pallas import tpu as pltpu
from jax.sharding import PartitionSpec as P

MESH = pl.DeviceIdType.MESH
BF = jnp.bfloat16
F32 = jnp.float32

HD = 128
HEADS = 16
CLIPS = 4
ROWS = 128
TOKENS = 2048
SLOT = TOKENS // CLIPS
D = 3072
PARTS = 2
SPLIT = 1
WIDE = D // PARTS
QB = 256
LOG2E = 1.4426950408889634
FACTOR = HD ** (-0.5)
SCALE = FACTOR * LOG2E


def rotary_layout(head_dim):
    quarter = head_dim // 4
    rest_span = (head_dim - quarter) // 2
    part_spans = (quarter, rest_span, head_dim - quarter - rest_span)
    partner, signs, axis_of, frequency = [], [], [], []
    offset = 0
    for part_index in range(3):
        part_span = part_spans[part_index]
        half_span = part_span // 2
        for inner_dim in range(part_span):
            pair_index = inner_dim % half_span
            if inner_dim < half_span:
                partner.append(offset + inner_dim + half_span)
                signs.append(-1.0)
            else:
                partner.append(offset + inner_dim - half_span)
                signs.append(1.0)
            axis_of.append(part_index)
            frequency.append(10000.0 ** (-pair_index / half_span))
        offset += part_span
    return np.array(partner), np.array(signs), np.array(axis_of), np.array(frequency)


def partner_matrix():
    partner, signs, _, _ = rotary_layout(HD)
    matrix = np.zeros((HD, HD), np.float32)
    matrix[partner, np.arange(HD)] = signs
    return matrix


def nt(left, right):
    return lax.dot_general(left, right, (((1,), (1,)), ((), ())), preferred_element_type=F32)


def nn(left, right):
    return jnp.dot(left, right, preferred_element_type=F32)


def al(index, size):
    return pl.multiple_of(index, size)


def finish(mixed_ref, gk_ref, gv_ref, gq_ref, zr_ref, cos_ref, sin_ref, perm_ref, mixed_out, gq_out, gk_out, gv_out, gw_out, wide, keys, values, sems):
    ways = ((mixed_ref, wide, mixed_out), (gk_ref, keys, gk_out), (gv_ref, values, gv_out))
    loads = [pltpu.make_async_copy(src, held, sems.at[i]) for i, (src, held, _) in enumerate(ways)]
    stores = [pltpu.make_async_copy(held, dst, sems.at[3 + i]) for i, (_, held, dst) in enumerate(ways)]
    for load in loads:
        load.start()
    for load, store in zip(loads, stores):
        load.wait()
        store.start()
    for h in range(HEADS):
        part = gq_ref[h]
        turned = part.astype(F32) * cos_ref[...] - nn(part, perm_ref[...]) * sin_ref[...]
        gq_out[:, h * HD : (h + 1) * HD] = turned.astype(BF)
    gw_out[...] = sum(zr_ref[i].astype(F32) for i in range(8))
    for store in stores:
        store.wait()


def kernel(
    q_hbm, k_hbm, v_hbm, cos_ref, sin_ref, perm_ref, w_hbm, cot_hbm, bucket_ref, cost_ref,
    mixed_hbm, gk_hbm, gv_hbm, gq_hbm, zr_hbm,
    q_ref, k_ref, v_ref, cot_ref, mixed_out, gk_out, gv_out,
    rin, rel, qh, kh, vh, kt, vt, wbuf, probs, ot, rl, att, dealt, att_tok,
    gd, gdh, dot_t, dq_t, gsend, grecv, cot_t, ct, at_all, gw_send, xr, zs, zr,
    ssem, rsem, lsem,
):
    dp, sp = lax.axis_index("dp"), lax.axis_index("sp")
    y, xl, c = dp // 4, (dp // 2) % 2, dp % 2
    z, xh = sp // 2, sp % 2
    x = xh * 2 + xl

    def device(x_, y_, z_, c_):
        return (y_ * 4 + (x_ % 2) * 2 + c_, z_ * 2 + x_ // 2)

    def send(src, dst, s, r, to):
        pltpu.make_async_remote_copy(
            src_ref=src, dst_ref=dst, send_sem=ssem.at[s], recv_sem=rsem.at[r],
            device_id=to, device_id_type=MESH,
        ).start()

    def keep(src, dst, r):
        pltpu.make_async_copy(src, dst, rsem.at[r]).start()

    def wait(view, sem):
        pltpu.make_async_copy(view, view, sem).wait()

    loads = [
        pltpu.make_async_copy(src, dst, lsem.at[i])
        for i, (src, dst) in enumerate(((cot_hbm, cot_ref), (q_hbm, q_ref), (k_hbm, k_ref), (v_hbm, v_ref)))
    ]
    for load in loads:
        load.start()

    barrier = pltpu.get_barrier_semaphore()

    def greet(to):
        pl.semaphore_signal(barrier, inc=1, device_id=to, device_id_type=MESH)

    @pl.loop(1, 16)
    def _(j):
        greet((dp, lax.rem(sp + j, 16)))

    @pl.loop(1, 8)
    def _(j):
        greet(device(x, (y + j // 2) % 4, z, (c + j) % 2))
        greet(device((x + j // 2) % 4, y, z, (c + j) % 2))

    pl.semaphore_wait(barrier, 29)

    def per_core(run):
        @pl.when(c == 0)
        def _():
            run(0, pl.ds(0, SPLIT))

        @pl.when(c == 1)
        def _():
            run(1, pl.ds(SPLIT, PARTS - SPLIT))

    def give_piece(core, parts):
        for t in range(parts.start, parts.start + parts.size):
            piece = w_hbm.at[pl.ds(al((y * 2 + xl) * 16, 16), 16), pl.ds(t * WIDE, WIDE)]
            spot = wbuf.at[t, xh, z, y, xl]
            keep(piece, spot, 8)

            @pl.loop(1, 8)
            def _(j, piece=piece, spot=spot):
                send(piece, spot, 8, 8, device(x, y, (z + j) % 8, c))

    per_core(give_piece)

    lanes = lambda h: pl.ds(al(h * HD, HD), HD)
    sibling = device(x, y, z, 1 - c)
    me8 = y * 2 + c
    loads[0].wait()
    for i in range(D // 128):
        cot_t[i * 128 : (i + 1) * 128, :] = cot_ref[:, i * 128 : (i + 1) * 128].T
    quarter = cot_t.at[pl.ds(al(y * 768, 768), 768)]
    keep(quarter, ct.at[:, lanes(me8)], 10)
    send(quarter, ct.at[:, lanes(me8)], 10, 10, sibling)
    for j in range(1, 4):
        ty = (y + j) % 4
        send(cot_t.at[pl.ds(al(ty * 768, 768), 768)], ct.at[:, lanes(me8)], 10, 36 + j, device(x, ty, z, c))

    def hand_over_cotangent():
        for j in range(1, 4):
            view = ct.at[:, lanes((y + 4 - j) % 4 * 2 + c)]
            wait(view, rsem.at[36 + j])
            send(view, view, 19, 10, sibling)

    cos, sin, perm = cos_ref[...], sin_ref[...], perm_ref[...]

    def turn(block, direction):
        return block.astype(F32) * cos + direction * nn(block, perm) * sin

    mine = pl.ds(al(sp * ROWS, ROWS), ROWS)

    partner = (dp, z * 2 + 1 - xh)
    theirs = pl.ds(al(partner[1] * ROWS, ROWS), ROWS)

    def fill(n, src, side):
        @pl.loop(0, 8)
        def _(i):
            part = src[:, lanes(i * 2 + side)]
            rin[n, side, i] = part if n == 2 else turn(part, 1.0).astype(BF)

    def cross(n):
        send(rin.at[n, 1 - xh], rel.at[n], 21 + n, 44 + n, partner)

    def along(n, view, dst, rows, s):
        keep(view.at[z], dst.at[rows], n)

        @pl.loop(1, 8)
        def _(j):
            tz = lax.rem(z + j, 8)
            send(view.at[tz], dst.at[rows], s, n, (dp, tz * 2 + xh))

    arrays = ((0, q_ref, qh), (1, k_ref, kh), (2, v_ref, vh))

    def hand_on(n, dst):
        wait(rel.at[n], rsem.at[44 + n])
        along(n, rel.at[n], dst, theirs, 24 + n)

    for n, src, _ in arrays[:2]:
        loads[1 + n].wait()
        fill(n, src, 1 - xh)
        cross(n)
    fill(0, q_ref, xh)
    along(0, rin.at[0, xh], qh, mine, 0)
    fill(1, k_ref, xh)
    loads[3].wait()
    fill(2, v_ref, xh)
    fill(2, v_ref, 1 - xh)

    def at(core, i, k):
        return ((x + 8 + i) % 4, (y + 8 + k) % 4) if core else ((x + 8 + k) % 4, (y + 8 + i) % 4)

    def block(core, parts, i, k):
        bx, by = at(core, i, k)
        return wbuf.at[parts, bx // 2, :, by, bx % 2]

    def half_of(core, parts, i, k, m):
        bx, by = at(core, i, k)
        return wbuf.at[parts, bx // 2, pl.ds(4 * m, 4), by, bx % 2]

    def ring_to(core, i, k):
        return device(*at(core, i, k), z, c)

    order = (0, -1, 1, 2)

    def share(core, parts, n):
        view = block(core, parts, order[n], 0)
        send(view, view, 14, 21 + 4 * n, ring_to(core, 0, 1))
        send(view, view, 14, 22 + 4 * n, ring_to(core, 0, -1))
        send(view, view, 13, 13, sibling)

    def pass_on(n):
        def run(core, parts):
            for side, m in ((-1, 0), (1, 1)):
                view = block(core, parts, order[n], side)
                part = half_of(core, parts, order[n], side, m)
                wait(view, rsem.at[21 + 4 * n + m])
                send(part, part, 15, 23 + 4 * n + m, ring_to(core, 0, -side))
                send(view, view, 13, 13, sibling)

        per_core(run)

    def first_ring_start(core, parts):
        own = block(core, parts, 0, 0)
        wait(own, rsem.at[8])
        send(own, own, 9, 17, ring_to(core, 1, 0))
        send(own, own, 9, 18, ring_to(core, -1, 0))
        share(core, parts, 0)

    def first_ring(core, parts):
        for n, side, m in ((1, -1, 0), (2, 1, 1)):
            part = half_of(core, parts, side, 0, m)
            wait(block(core, parts, side, 0), rsem.at[17 + m])
            send(part, part, 16, 19 + m, ring_to(core, -side, 0))
            share(core, parts, n)

    def first_ring_end(core, parts):
        for m in range(2):
            wait(half_of(core, parts, 2, 0, m), rsem.at[19 + m])
        share(core, parts, 3)

    def second_ring_end(core, parts):
        for n in range(4):
            for m in range(2):
                wait(half_of(core, parts, order[n], 2, m), rsem.at[23 + 4 * n + m])
            view = block(core, parts, order[n], 2)
            send(view, view, 13, 13, sibling)

    def others_come(core, parts):
        rest = pl.ds(0, SPLIT) if core else pl.ds(SPLIT, PARTS - SPLIT)
        wait(wbuf.at[rest], rsem.at[13])

    per_core(first_ring_start)
    along(1, rin.at[1, xh], kh, mine, 1)
    for n, _, dst in arrays[:2]:
        hand_on(n, dst)
    along(2, rin.at[2, xh], vh, mine, 2)
    per_core(first_ring)
    cross(2)
    hand_over_cotangent()
    pass_on(0)
    per_core(first_ring_end)
    hand_on(2, vh)
    pass_on(1)

    wait(qh, rsem.at[0])
    wait(kh, rsem.at[1])
    narrow = jnp.where(bucket_ref[0] == 1, 0.0, -1e30).astype(F32)

    def weigh(b):
        cols = pl.ds(al(b * QB, QB), QB)
        slot = b // (SLOT // QB)
        scores = nt(kh[...], qh[cols, :])
        parts = [scores[i * SLOT : (i + 1) * SLOT] for i in range(CLIPS)]
        masks = [jnp.where(slot == i, 0.0, narrow) for i in range(CLIPS)]
        tops = [jnp.max(part, axis=0, keepdims=True) + mask for part, mask in zip(parts, masks)]
        top = functools.reduce(jnp.maximum, tops) * SCALE
        for i in range(CLIPS):
            low = jnp.exp2(parts[i] * SCALE - (top - masks[i])).astype(BF)
            probs[i * SLOT : (i + 1) * SLOT, cols] = low

    pl.loop(0, 4)(weigh)
    pass_on(2)
    pl.loop(4, TOKENS // QB)(weigh)
    pass_on(3)

    wait(vh, rsem.at[2])
    vt[:HD, :] = vh[...].T
    vt[HD:, :] = jnp.ones((16, TOKENS), BF)

    @pl.loop(0, TOKENS // QB)
    def _(b):
        cols = pl.ds(al(b * QB, QB), QB)
        out = nn(vt[...], probs[:, cols])
        scale = 1.0 / out[HD : HD + 1]
        rl[:, cols] = scale
        out = out[:HD] * scale
        ot[:, cols] = out
        att[cols, :] = out.T.astype(BF)

    costs = [cost_ref[0, k] for k in range(CLIPS)]
    wide = bucket_ref[0] == 1
    rank = []
    for k in range(CLIPS):
        count = jnp.int32(0)
        for j in range(CLIPS):
            if j != k:
                above = costs[j] >= costs[k] if j < k else costs[j] > costs[k]
                count = count + jnp.where(above, 1, 0)
        rank.append(jnp.where(wide, k, count))
    choose = [[jnp.where(rank[k] == r, 1.0, 0.0).astype(F32) for k in range(CLIPS)] for r in range(CLIPS)]

    slots = [att[k * SLOT : (k + 1) * SLOT, :].astype(F32) for k in range(CLIPS)]
    for r in range(CLIPS):
        picked = sum(slots[k] * choose[r][k] for k in range(CLIPS))
        dealt[r * SLOT : (r + 1) * SLOT, :] = picked.astype(BF)

    here = att_tok.at[xh, :, lanes(z)]
    keep(dealt.at[mine], here, 3)

    @pl.loop(1, 16)
    def _(j):
        t = lax.rem(sp + j, 16)
        send(dealt.at[pl.ds(al(t * ROWS, ROWS), ROWS)], here, 3, 3, (dp, t))

    per_core(second_ring_end)

    per_core(others_come)

    def grad_of(h):
        total = sum(
            nt(cot_ref[:, t * WIDE : (t + 1) * WIDE], wbuf[t, h % 2, h // 2].reshape(HD, WIDE))
            for t in range(PARTS)
        )
        gd[h] = total.astype(BF)

    grad_of(sp)
    keep(gd.at[sp], gdh.at[mine], 4)

    @pl.loop(1, 16)
    def _(j):
        h = lax.rem(sp + j, 16)
        grad_of(h)
        send(gd.at[h], gdh.at[mine], 4, 4, (dp, h))

    wait(att_tok, rsem.at[3])
    def rows_of(ty, tc, first=0, count=ROWS):
        return at_all.at[pl.ds(al((ty * 2 + tc) * ROWS + first, count), count)]

    at_here = rows_of(y, c)
    keep(att_tok.at[c], at_here, 11)
    for tc in range(2):
        send(att_tok.at[tc], at_here, 11, 40 + c, device(x, (y + 1) % 4, z, tc))
        send(att_tok.at[tc], at_here, 11, 42 + c, device(x, (y + 3) % 4, z, tc))
    send(att_tok.at[1 - c], at_here, 11, 11, sibling)

    for t in range(PARTS):

        @pl.loop(0, WIDE // 512)
        def _(i, t=t):
            cols = pl.ds(al(i * 512, 512), 512)
            total = nn(att_tok[0], wbuf[t, 0, :, :, :, :, cols].reshape(1024, 512))
            total += nn(att_tok[1], wbuf[t, 1, :, :, :, :, cols].reshape(1024, 512))
            mixed_out[:, pl.ds(al(t * WIDE + i * 512, 512), 512)] = total.astype(BF)

    stores = [
        pltpu.make_async_copy(src, dst, lsem.at[4 + i])
        for i, (src, dst) in enumerate(
            ((mixed_out, mixed_hbm), (gv_out, gv_hbm), (gk_out, gk_hbm), (grecv.at[2], gq_hbm), (zr, zr_hbm))
        )
    ]
    stores[0].start()

    for m, step in ((0, 3), (1, 1)):
        ty = (y + step) % 4
        for tc in range(2):
            wait(rows_of(ty, tc), rsem.at[40 + 2 * m + tc])
            part = rows_of(ty, tc, 64 * m, 64)
            send(part, part, 18, 11, device(x, (y + 4 - step) % 4, z, c))

    kt[...] = kh[...].T

    wait(gdh, rsem.at[4])
    slots = [gdh[k * SLOT : (k + 1) * SLOT, :].astype(F32) for k in range(CLIPS)]
    for k in range(CLIPS):
        picked = sum(slots[r] * choose[r][k] for r in range(CLIPS))
        part = slice(k * SLOT, (k + 1) * SLOT)
        dot_t[:, part] = (picked.T * rl[:, part]).astype(BF)

    def give(n, t):
        @pl.when(t == sp)
        def _():
            keep(gsend.at[n, t], grecv.at[n, sp], 5 + n)

        @pl.when(t != sp)
        def _():
            send(gsend.at[n, t], grecv.at[n, sp], 5 + n, 5 + n, (dp, t))

    centre = jnp.sum(dot_t[...].astype(F32) * ot[...], axis=0, keepdims=True)

    @pl.loop(0, TOKENS // QB)
    def _(i):
        b = (i + sp // 2) % (TOKENS // QB)
        rows = pl.ds(al(b * QB, QB), QB)
        low = probs[rows, :]
        value_grad = nt(low, dot_t[...]).astype(BF)
        gsend[0, b * 2] = value_grad[:ROWS]
        gsend[0, b * 2 + 1] = value_grad[ROWS:]
        give(0, b * 2)
        give(0, b * 2 + 1)

    wait(ct.at[:, pl.ds(0, 5 * HD)], rsem.at[10])
    wait(at_all.at[pl.ds(0, 4 * ROWS)], rsem.at[11])
    for b in range(4):
        gw_send[b] = nn(ct[b * 192 : (b + 1) * 192, :], at_all[...]).astype(BF)
        tx, tc = 2 * c + b // 2, b % 2
        same = jnp.logical_and(tx == x, tc == c)

        @pl.when(same)
        def _(b=b):
            keep(gw_send.at[b], xr.at[x], 12)

        @pl.when(jnp.logical_not(same))
        def _(b=b, tx=tx, tc=tc):
            send(gw_send.at[b], xr.at[x], 12, 12, device(tx, y, z, tc))

    dq_t[...] = jnp.zeros_like(dq_t)

    @pl.loop(0, TOKENS // QB)
    def _(i):
        b = (i + sp // 2) % (TOKENS // QB)
        rows = pl.ds(al(b * QB, QB), QB)
        grad_probs = nn(vh[rows, :], dot_t[...])
        grad_scores = (probs[rows, :].astype(F32) * (grad_probs - centre)).astype(BF)
        key_grad = (nn(grad_scores, qh[...]) * FACTOR).astype(BF)
        gsend[1, b * 2] = key_grad[:ROWS]
        gsend[1, b * 2 + 1] = key_grad[ROWS:]
        give(1, b * 2)
        give(1, b * 2 + 1)
        dq_t[...] += nn(kt[:, rows], grad_scores)

    @pl.loop(0, HEADS)
    def _(i):
        t = lax.rem(sp + i, 16)
        gsend[2, t] = (dq_t[:, lanes(t)].T * FACTOR).astype(BF)
        give(2, t)

    wait(xr, rsem.at[12])
    for i in range(8):
        cols = slice(i * HD, (i + 1) * HD)
        total = sum(xr[j, :, cols].astype(F32) for j in range(4))
        zs[i] = total.astype(BF)
    keep(zs.at[z], zr.at[z], 9)

    @pl.loop(1, 8)
    def _(j):
        tz = (z + j) % 8
        send(zs.at[tz], zr.at[z], 17, 9, device(x, y, tz, c))

    wait(grecv.at[0], rsem.at[5])
    for h in range(HEADS):
        gv_out[:, h * HD : (h + 1) * HD] = grecv[0, h]
    stores[1].start()
    wait(grecv.at[1], rsem.at[6])

    @pl.loop(0, HEADS)
    def _(h):
        gk_out[:, lanes(h)] = turn(grecv[1, h], -1.0).astype(BF)

    stores[2].start()
    wait(zr, rsem.at[9])
    stores[4].start()
    wait(grecv.at[2], rsem.at[7])
    stores[3].start()

    for store in stores:
        store.wait()
    most = lambda ref: ref.at[pl.ds(0, 15)]
    for n in range(3):
        wait(rel.at[n, pl.ds(0, 7)], ssem.at[n])
        wait(rel.at[n], ssem.at[21 + n])
        wait(rel.at[n, pl.ds(0, 7)], ssem.at[24 + n])
    wait(most(gd), ssem.at[3])
    wait(most(gd), ssem.at[4])
    for n in range(3):
        wait(most(gsend.at[n]), ssem.at[5 + n])

    def weights_left(core, parts):
        wait(wbuf.at[parts, 0, pl.ds(0, 7), 0, 0], ssem.at[8])
        wait(wbuf.at[parts], ssem.at[13])
        wait(wbuf.at[parts, 0, :, 0, :], ssem.at[9])
        wait(wbuf.at[parts, 0, :, 0, 0], ssem.at[16])
        wait(wbuf.at[parts, 0], ssem.at[14])
        wait(wbuf.at[parts, 0, :, :, 0], ssem.at[15])

    per_core(weights_left)
    wait(zs.at[pl.ds(0, 7)], ssem.at[17])
    wait(ct.at[:, pl.ds(0, 4 * HD)], ssem.at[10])
    wait(ct.at[:, pl.ds(0, 3 * HD)], ssem.at[19])
    wait(at_all.at[pl.ds(0, 5 * ROWS)], ssem.at[11])
    wait(at_all.at[pl.ds(0, 2 * ROWS)], ssem.at[18])
    wait(gw_send.at[pl.ds(0, 3)], ssem.at[12])

    @pl.when(c != xh)
    def _():
        wait(gw_send.at[0], ssem.at[12])


def local(query, key_in, value, bucket, clip_cost, positions, out_weight, cotangent):
    _, _, axis_of, frequency = rotary_layout(HD)
    angles = jnp.transpose(positions[:, 0, :].astype(F32))
    angles = jnp.concatenate(
        [jnp.broadcast_to(angles[:, a : a + 1], (ROWS, int(np.sum(axis_of == a)))) for a in range(3)], axis=1
    ) * jnp.asarray(frequency, F32)
    perm = jnp.asarray(partner_matrix(), BF)

    vmem = pl.BlockSpec(memory_space=pltpu.VMEM)
    smem = pl.BlockSpec(memory_space=pltpu.SMEM)
    bf = lambda *shape: pltpu.VMEM(shape, BF)
    f32 = lambda *shape: pltpu.VMEM(shape, F32)
    shape = jax.ShapeDtypeStruct
    hbm = pl.BlockSpec(memory_space=pl.ANY)
    cos, sin = jnp.cos(angles), jnp.sin(angles)
    rows = shape((ROWS, TOKENS), BF)
    mixed, grad_key, grad_value, raw_query, terms = pl.pallas_call(
        kernel,
        out_shape=(shape((ROWS, D), BF), rows, rows, shape((16, ROWS, HD), BF), shape((8, 192, HD), BF)),
        in_specs=[hbm] * 3 + [vmem] * 3 + [hbm] * 2 + [smem] * 2,
        out_specs=(hbm,) * 5,
        scratch_shapes=[
            bf(ROWS, TOKENS), bf(ROWS, TOKENS), bf(ROWS, TOKENS), bf(ROWS, D),
            bf(ROWS, D), bf(ROWS, TOKENS), bf(ROWS, TOKENS),
            bf(3, 2, 8, ROWS, HD), bf(3, 8, ROWS, HD),
            bf(TOKENS, HD), bf(TOKENS, HD), bf(TOKENS, HD),
            bf(HD, TOKENS), bf(HD + 16, TOKENS),
            bf(PARTS, 2, 8, 4, 2, 16, WIDE),
            bf(TOKENS, TOKENS),
            f32(HD, TOKENS), f32(1, TOKENS),
            bf(TOKENS, HD), bf(TOKENS, HD),
            bf(2, ROWS, 1024),
            bf(16, ROWS, HD), bf(TOKENS, HD),
            bf(HD, TOKENS), f32(HD, TOKENS),
            bf(3, 16, ROWS, HD), bf(3, 16, ROWS, HD),
            bf(D, ROWS), bf(768, 1024), bf(1024, 1024),
            bf(4, 192, 1024), bf(4, 192, 1024),
            bf(8, 192, HD), bf(8, 192, HD),
            pltpu.SemaphoreType.DMA((27,)), pltpu.SemaphoreType.DMA((47,)), pltpu.SemaphoreType.DMA((9,)),
        ],
        compiler_params=pltpu.CompilerParams(
            collective_id=0, has_side_effects=True, vmem_limit_bytes=62 * 2**20
        ),
    )(
        query[0], key_in[0], value[0], cos, sin, perm,
        out_weight, cotangent[0], bucket, clip_cost,
    )
    mixed, grad_query, grad_key, grad_value, grad_weight = pl.pallas_call(
        finish,
        out_shape=(shape((ROWS, D), BF), rows, rows, rows, shape((192, HD), F32)),
        in_specs=[hbm] * 3 + [vmem] * 5,
        out_specs=(hbm, vmem, hbm, hbm, vmem),
        scratch_shapes=[bf(ROWS, D), bf(ROWS, TOKENS), bf(ROWS, TOKENS), pltpu.SemaphoreType.DMA((6,))],
    )(mixed, grad_key, grad_value, raw_query, terms, cos, sin, perm)
    return mixed[None], grad_query[None], grad_key[None], grad_value[None], grad_weight.T


def solution(mesh):
    in_specs = (
        P("dp", "sp", None),
        P("dp", "sp", None),
        P("dp", "sp", None),
        P("dp"),
        P("dp", None),
        P(None, "dp", "sp"),
        P("sp", None),
        P("dp", "sp", None),
    )
    out_specs = (
        P("dp", "sp", None),
        P("dp", "sp", None),
        P("dp", "sp", None),
        P("dp", "sp", None),
        P("sp", "dp"),
    )
    return jax.shard_map(local, mesh=mesh, in_specs=in_specs, out_specs=out_specs, check_vma=False)
```

```python
import functools

import jax
import jax.numpy as jnp
import numpy as np
from jax import lax
from jax.experimental import pallas as pl
from jax.experimental.pallas import tpu as pltpu
from jax.sharding import PartitionSpec as P

MESH = pl.DeviceIdType.MESH
BF = jnp.bfloat16
F32 = jnp.float32

HD = 128
HEADS = 16
CLIPS = 4
ROWS = 128
TOKENS = 2048
SLOT = TOKENS // CLIPS
D = 3072
PARTS = 2
SPLIT = 1
WIDE = D // PARTS
QB = 256
LOG2E = 1.4426950408889634
FACTOR = HD ** (-0.5)
SCALE = FACTOR * LOG2E


def rotary_layout(head_dim):
    quarter = head_dim // 4
    rest_span = (head_dim - quarter) // 2
    part_spans = (quarter, rest_span, head_dim - quarter - rest_span)
    partner, signs, axis_of, frequency = [], [], [], []
    offset = 0
    for part_index in range(3):
        part_span = part_spans[part_index]
        half_span = part_span // 2
        for inner_dim in range(part_span):
            pair_index = inner_dim % half_span
            if inner_dim < half_span:
                partner.append(offset + inner_dim + half_span)
                signs.append(-1.0)
            else:
                partner.append(offset + inner_dim - half_span)
                signs.append(1.0)
            axis_of.append(part_index)
            frequency.append(10000.0 ** (-pair_index / half_span))
        offset += part_span
    return np.array(partner), np.array(signs), np.array(axis_of), np.array(frequency)


def partner_matrix():
    partner, signs, _, _ = rotary_layout(HD)
    matrix = np.zeros((HD, HD), np.float32)
    matrix[partner, np.arange(HD)] = signs
    return matrix


def nt(left, right):
    return lax.dot_general(left, right, (((1,), (1,)), ((), ())), preferred_element_type=F32)


def nn(left, right):
    return jnp.dot(left, right, preferred_element_type=F32)


def al(index, size):
    return pl.multiple_of(index, size)


def finish(
    mixed_hbm, gk_hbm, gv_hbm, raw_hbm, terms_hbm, cos_hbm, sin_hbm, perm_hbm,
    mixed_out, gq_out, gk_out, gv_out, gw_out,
    mixed, gk, gv, raw, terms, cos, sin, perm, gq, gw, load_sem, store_sem,
):
    pairs = (
        (raw_hbm, raw), (cos_hbm, cos), (sin_hbm, sin), (perm_hbm, perm), (terms_hbm, terms),
        (mixed_hbm, mixed), (gk_hbm, gk), (gv_hbm, gv),
    )
    loads = [pltpu.make_async_copy(src, dst, load_sem.at[i]) for i, (src, dst) in enumerate(pairs)]
    pairs = ((gq, gq_out), (gw, gw_out), (mixed, mixed_out), (gk, gk_out), (gv, gv_out))
    stores = [pltpu.make_async_copy(src, dst, store_sem.at[i]) for i, (src, dst) in enumerate(pairs)]
    for load in loads:
        load.start()
    for load in loads[:4]:
        load.wait()
    for h in range(HEADS):
        part = raw[h]
        turned = part.astype(F32) * cos[...] - nn(part, perm[...]) * sin[...]
        gq[:, h * HD : (h + 1) * HD] = turned.astype(BF)
    stores[0].start()
    for load, store in zip(loads[5:], stores[2:]):
        load.wait()
        store.start()
    loads[4].wait()
    gw[...] = sum(terms[i].astype(F32) for i in range(8))
    stores[1].start()
    for store in stores:
        store.wait()


def kernel(
    q_hbm, k_hbm, v_hbm, pos_ref, freq_ref, perm_ref, w_hbm, cot_hbm, bucket_ref, cost_ref,
    mixed_hbm, gk_hbm, gv_hbm, gq_hbm, zr_hbm, cos_hbm, sin_hbm,
    cos_ref, sin_ref,
    q_ref, k_ref, v_ref, cot_ref, mixed_out, gk_out, gv_out,
    rin, rel, qh, kh, vh, kt, vt, wbuf, probs, ot, rl, att, dealt, att_tok,
    gd, gdh, dot_t, dq_t, gsend, grecv, cot_t, ct, at_all, gw_send, xr, zs, zr,
    ssem, rsem, lsem,
):
    dp, sp = lax.axis_index("dp"), lax.axis_index("sp")
    y, xl, c = dp // 4, (dp // 2) % 2, dp % 2
    z, xh = sp // 2, sp % 2
    x = xh * 2 + xl

    def device(x_, y_, z_, c_):
        return (y_ * 4 + (x_ % 2) * 2 + c_, z_ * 2 + x_ // 2)

    def send(src, dst, s, r, to):
        pltpu.make_async_remote_copy(
            src_ref=src, dst_ref=dst, send_sem=ssem.at[s], recv_sem=rsem.at[r],
            device_id=to, device_id_type=MESH,
        ).start()

    def keep(src, dst, r):
        pltpu.make_async_copy(src, dst, rsem.at[r]).start()

    def wait(view, sem):
        pltpu.make_async_copy(view, view, sem).wait()

    loads = [
        pltpu.make_async_copy(src, dst, lsem.at[i])
        for i, (src, dst) in enumerate(((cot_hbm, cot_ref), (q_hbm, q_ref), (k_hbm, k_ref), (v_hbm, v_ref)))
    ]
    for load in loads:
        load.start()

    vt[HD:, :] = jnp.ones((16, TOKENS), BF)

    barrier = pltpu.get_barrier_semaphore()

    def greet(to):
        pl.semaphore_signal(barrier, inc=1, device_id=to, device_id_type=MESH)

    @pl.loop(1, 16)
    def _(j):
        greet((dp, lax.rem(sp + j, 16)))

    @pl.loop(1, 8)
    def _(j):
        greet(device(x, (y + j // 2) % 4, z, (c + j) % 2))
        greet(device((x + j // 2) % 4, y, z, (c + j) % 2))

    pl.semaphore_wait(barrier, 29)

    def per_core(run):
        @pl.when(c == 0)
        def _():
            run(0, pl.ds(0, SPLIT))

        @pl.when(c == 1)
        def _():
            run(1, pl.ds(SPLIT, PARTS - SPLIT))

    def give_piece(core, parts):
        for t in range(parts.start, parts.start + parts.size):
            piece = w_hbm.at[pl.ds(al((y * 2 + xl) * 16, 16), 16), pl.ds(t * WIDE, WIDE)]
            spot = wbuf.at[t, xh, z, y, xl]
            keep(piece, spot, 8)

            @pl.loop(1, 8)
            def _(j, piece=piece, spot=spot):
                send(piece, spot, 8, 8, device(x, y, (z + j) % 8, c))

    per_core(give_piece)

    lanes = lambda h: pl.ds(al(h * HD, HD), HD)
    sibling = device(x, y, z, 1 - c)
    me8 = y * 2 + c

    def hand_over_cotangent():
        for j in range(1, 4):
            view = ct.at[:, lanes((y + 4 - j) % 4 * 2 + c)]
            wait(view, rsem.at[36 + j])
            send(view, view, 19, 10, sibling)

    angles = sum(
        jnp.broadcast_to(pos_ref[a].astype(F32), (ROWS, ROWS)).T * freq_ref[a : a + 1] for a in range(3)
    )
    cos_ref[...] = jnp.cos(angles)
    sin_ref[...] = jnp.sin(angles)

    cos, sin, perm = cos_ref[...], sin_ref[...], perm_ref[...]

    def turn(block, direction):
        return block.astype(F32) * cos + direction * nn(block, perm) * sin

    mine = pl.ds(al(sp * ROWS, ROWS), ROWS)

    partner = (dp, z * 2 + 1 - xh)
    theirs = pl.ds(al(partner[1] * ROWS, ROWS), ROWS)

    def fill(n, src, side):
        @pl.loop(0, 8)
        def _(i):
            part = src[:, lanes(i * 2 + side)]
            rin[n, side, i] = part.T if n == 2 else turn(part, 1.0).astype(BF)

    def cross(n):
        send(rin.at[n, 1 - xh], rel.at[n], 21 + n, 44 + n, partner)

    def along(n, view, dst, rows, s):
        spot = dst.at[pl.ds(0, HD), rows] if n == 2 else dst.at[rows]
        keep(view.at[z], spot, n)

        @pl.loop(1, 8)
        def _(j):
            tz = lax.rem(z + j, 8)
            send(view.at[tz], spot, s, n, (dp, tz * 2 + xh))

    arrays = ((0, q_ref, qh), (1, k_ref, kh), (2, v_ref, vt))

    def hand_on(n, dst):
        wait(rel.at[n], rsem.at[44 + n])
        along(n, rel.at[n], dst, theirs, 24 + n)

    for n, src, _ in arrays[:2]:
        loads[1 + n].wait()
        fill(n, src, 1 - xh)
        cross(n)
    fill(0, q_ref, xh)
    along(0, rin.at[0, xh], qh, mine, 0)

    loads[0].wait()
    for i in range(D // 128):
        cot_t[i * 128 : (i + 1) * 128, :] = cot_ref[:, i * 128 : (i + 1) * 128].T
    quarter = cot_t.at[pl.ds(al(y * 768, 768), 768)]
    keep(quarter, ct.at[:, lanes(me8)], 10)
    send(quarter, ct.at[:, lanes(me8)], 10, 10, sibling)
    for j in range(1, 4):
        ty = (y + j) % 4
        send(cot_t.at[pl.ds(al(ty * 768, 768), 768)], ct.at[:, lanes(me8)], 10, 36 + j, device(x, ty, z, c))

    fill(1, k_ref, xh)
    loads[3].wait()
    fill(2, v_ref, xh)
    fill(2, v_ref, 1 - xh)

    def at(core, i, k):
        return ((x + 8 + i) % 4, (y + 8 + k) % 4) if core else ((x + 8 + k) % 4, (y + 8 + i) % 4)

    def block(core, parts, i, k):
        bx, by = at(core, i, k)
        return wbuf.at[parts, bx // 2, :, by, bx % 2]

    def half_of(core, parts, i, k, m):
        bx, by = at(core, i, k)
        return wbuf.at[parts, bx // 2, pl.ds(4 * m, 4), by, bx % 2]

    def ring_to(core, i, k):
        return device(*at(core, i, k), z, c)

    order = (0, -1, 1, 2)

    def share(core, parts, n):
        view = block(core, parts, order[n], 0)
        send(view, view, 14, 21 + 4 * n, ring_to(core, 0, 1))
        send(view, view, 14, 22 + 4 * n, ring_to(core, 0, -1))
        send(view, view, 13, 13, sibling)

    def pass_on(n):
        def run(core, parts):
            for side, m in ((-1, 0), (1, 1)):
                view = block(core, parts, order[n], side)
                part = half_of(core, parts, order[n], side, m)
                wait(view, rsem.at[21 + 4 * n + m])
                send(part, part, 15, 23 + 4 * n + m, ring_to(core, 0, -side))
                send(view, view, 13, 13, sibling)

        per_core(run)

    def first_ring_start(core, parts):
        own = block(core, parts, 0, 0)
        wait(own, rsem.at[8])
        send(own, own, 9, 17, ring_to(core, 1, 0))
        send(own, own, 9, 18, ring_to(core, -1, 0))
        share(core, parts, 0)

    def first_ring(core, parts):
        for n, side, m in ((1, -1, 0), (2, 1, 1)):
            part = half_of(core, parts, side, 0, m)
            wait(block(core, parts, side, 0), rsem.at[17 + m])
            send(part, part, 16, 19 + m, ring_to(core, -side, 0))
            share(core, parts, n)

    def first_ring_end(core, parts):
        for m in range(2):
            wait(half_of(core, parts, 2, 0, m), rsem.at[19 + m])
        share(core, parts, 3)

    def second_ring_end(core, parts):
        for n in range(4):
            for m in range(2):
                wait(half_of(core, parts, order[n], 2, m), rsem.at[23 + 4 * n + m])
            view = block(core, parts, order[n], 2)
            send(view, view, 13, 13, sibling)

    def others_come(core, parts):
        rest = pl.ds(0, SPLIT) if core else pl.ds(SPLIT, PARTS - SPLIT)
        wait(wbuf.at[rest], rsem.at[13])

    per_core(first_ring_start)
    along(1, rin.at[1, xh], kh, mine, 1)
    for n, _, dst in arrays[:2]:
        hand_on(n, dst)
    along(2, rin.at[2, xh], vt, mine, 2)
    per_core(first_ring)
    cross(2)
    hand_over_cotangent()
    pass_on(0)
    per_core(first_ring_end)
    hand_on(2, vt)
    pass_on(1)

    wait(qh, rsem.at[0])
    wait(kh, rsem.at[1])
    narrow = jnp.where(bucket_ref[0] == 1, 0.0, -1e30).astype(F32)

    def weigh(b):
        cols = pl.ds(al(b * QB, QB), QB)
        slot = b // (SLOT // QB)
        scores = nt(kh[...], qh[cols, :])
        parts = [scores[i * SLOT : (i + 1) * SLOT] for i in range(CLIPS)]
        masks = [jnp.where(slot == i, 0.0, narrow) for i in range(CLIPS)]
        tops = [jnp.max(part, axis=0, keepdims=True) + mask for part, mask in zip(parts, masks)]
        top = functools.reduce(jnp.maximum, tops) * SCALE
        for i in range(CLIPS):
            low = jnp.exp2(parts[i] * SCALE - (top - masks[i])).astype(BF)
            probs[i * SLOT : (i + 1) * SLOT, cols] = low

    pl.loop(0, 4)(weigh)
    pass_on(2)
    pl.loop(4, TOKENS // QB)(weigh)
    pass_on(3)

    wait(vt.at[pl.ds(0, HD)], rsem.at[2])

    @pl.loop(0, TOKENS // QB)
    def _(b):
        cols = pl.ds(al(b * QB, QB), QB)
        out = nn(vt[...], probs[:, cols])
        scale = 1.0 / out[HD : HD + 1]
        rl[:, cols] = scale
        out = out[:HD] * scale
        ot[:, cols] = out
        att[cols, :] = out.T.astype(BF)

    costs = [cost_ref[0, k] for k in range(CLIPS)]
    wide = bucket_ref[0] == 1
    rank = []
    for k in range(CLIPS):
        count = jnp.int32(0)
        for j in range(CLIPS):
            if j != k:
                above = costs[j] >= costs[k] if j < k else costs[j] > costs[k]
                count = count + jnp.where(above, 1, 0)
        rank.append(jnp.where(wide, k, count))
    choose = [[jnp.where(rank[k] == r, 1.0, 0.0).astype(F32) for k in range(CLIPS)] for r in range(CLIPS)]

    slots = [att[k * SLOT : (k + 1) * SLOT, :].astype(F32) for k in range(CLIPS)]
    for r in range(CLIPS):
        picked = sum(slots[k] * choose[r][k] for k in range(CLIPS))
        dealt[r * SLOT : (r + 1) * SLOT, :] = picked.astype(BF)

    here = att_tok.at[xh, :, lanes(z)]
    keep(dealt.at[mine], here, 3)

    @pl.loop(1, 16)
    def _(j):
        t = lax.rem(sp + j, 16)
        send(dealt.at[pl.ds(al(t * ROWS, ROWS), ROWS)], here, 3, 3, (dp, t))

    per_core(second_ring_end)

    per_core(others_come)

    def grad_of(h):
        total = sum(
            nt(wbuf[t, h % 2, h // 2].reshape(HD, WIDE), cot_ref[:, t * WIDE : (t + 1) * WIDE])
            for t in range(PARTS)
        )
        gd[h] = total.astype(BF)

    grad_of(sp)
    keep(gd.at[sp], gdh.at[:, mine], 4)

    @pl.loop(0, 15)
    def _(j):
        h = lax.rem(sp + 1 + lax.rem(j + 7, 15), 16)
        grad_of(h)
        send(gd.at[h], gdh.at[:, mine], 4, 4, (dp, h))

    wait(att_tok, rsem.at[3])
    def rows_of(ty, tc, first=0, count=ROWS):
        return at_all.at[pl.ds(al((ty * 2 + tc) * ROWS + first, count), count)]

    at_here = rows_of(y, c)
    keep(att_tok.at[c], at_here, 11)
    for tc in range(2):
        send(att_tok.at[tc], at_here, 11, 40 + c, device(x, (y + 1) % 4, z, tc))
        send(att_tok.at[tc], at_here, 11, 42 + c, device(x, (y + 3) % 4, z, tc))
    send(att_tok.at[1 - c], at_here, 11, 11, sibling)

    for t in range(PARTS):

        @pl.loop(0, WIDE // 512)
        def _(i, t=t):
            cols = pl.ds(al(i * 512, 512), 512)
            total = nn(att_tok[0], wbuf[t, 0, :, :, :, :, cols].reshape(1024, 512))
            total += nn(att_tok[1], wbuf[t, 1, :, :, :, :, cols].reshape(1024, 512))
            mixed_out[:, pl.ds(al(t * WIDE + i * 512, 512), 512)] = total.astype(BF)

    stores = [
        pltpu.make_async_copy(src, dst, lsem.at[4 + i])
        for i, (src, dst) in enumerate(
            (
                (mixed_out, mixed_hbm), (gv_out, gv_hbm), (gk_out, gk_hbm), (grecv.at[2], gq_hbm), (zr, zr_hbm),
                (cos_ref, cos_hbm), (sin_ref, sin_hbm),
            )

        )
    ]
    for store in (stores[0], stores[5], stores[6]):
        store.start()

    for m, step in ((0, 3), (1, 1)):
        ty = (y + step) % 4
        for tc in range(2):
            wait(rows_of(ty, tc), rsem.at[40 + 2 * m + tc])
            part = rows_of(ty, tc, 64 * m, 64)
            send(part, part, 18, 11, device(x, (y + 4 - step) % 4, z, c))

    kt[...] = kh[...].T
    vh[...] = vt[:HD, :].T

    wait(gdh, rsem.at[4])
    slots = [gdh[:, k * SLOT : (k + 1) * SLOT].astype(F32) for k in range(CLIPS)]
    for k in range(CLIPS):
        picked = sum(slots[r] * choose[r][k] for r in range(CLIPS))
        part = slice(k * SLOT, (k + 1) * SLOT)
        dot_t[:, part] = (picked * rl[:, part]).astype(BF)

    def give(n, t):
        @pl.when(t == sp)
        def _():
            keep(gsend.at[n, t], grecv.at[n, sp], 5 + n)

        @pl.when(t != sp)
        def _():
            send(gsend.at[n, t], grecv.at[n, sp], 5 + n, 5 + n, (dp, t))

    centre = jnp.sum(dot_t[...].astype(F32) * ot[...], axis=0, keepdims=True)

    @pl.loop(0, TOKENS // QB)
    def _(i):
        b = (i + sp // 2 + 4) % (TOKENS // QB)
        rows = pl.ds(al(b * QB, QB), QB)
        low = probs[rows, :]
        value_grad = nt(low, dot_t[...]).astype(BF)
        gsend[0, b * 2] = value_grad[:ROWS]
        gsend[0, b * 2 + 1] = value_grad[ROWS:]
        give(0, b * 2)
        give(0, b * 2 + 1)

    wait(ct.at[:, pl.ds(0, 5 * HD)], rsem.at[10])
    wait(at_all.at[pl.ds(0, 4 * ROWS)], rsem.at[11])
    for b in range(4):
        gw_send[b] = nn(ct[b * 192 : (b + 1) * 192, :], at_all[...]).astype(BF)
        tx, tc = 2 * c + b // 2, b % 2
        same = jnp.logical_and(tx == x, tc == c)

        @pl.when(same)
        def _(b=b):
            keep(gw_send.at[b], xr.at[x], 12)

        @pl.when(jnp.logical_not(same))
        def _(b=b, tx=tx, tc=tc):
            send(gw_send.at[b], xr.at[x], 12, 12, device(tx, y, z, tc))

    dq_t[...] = jnp.zeros_like(dq_t)

    @pl.loop(0, TOKENS // QB)
    def _(i):
        b = (i + sp // 2) % (TOKENS // QB)
        rows = pl.ds(al(b * QB, QB), QB)
        grad_probs = nn(vh[rows, :], dot_t[...])
        grad_scores = (probs[rows, :].astype(F32) * (grad_probs - centre)).astype(BF)
        key_grad = (nn(grad_scores, qh[...]) * FACTOR).astype(BF)
        gsend[1, b * 2] = key_grad[:ROWS]
        gsend[1, b * 2 + 1] = key_grad[ROWS:]
        give(1, b * 2)
        give(1, b * 2 + 1)
        dq_t[...] += nn(kt[:, rows], grad_scores)

    @pl.loop(0, HEADS)
    def _(i):
        t = lax.rem(sp + i, 16)
        gsend[2, t] = (dq_t[:, lanes(t)].T * FACTOR).astype(BF)
        give(2, t)

    wait(xr, rsem.at[12])
    for i in range(8):
        cols = slice(i * HD, (i + 1) * HD)
        total = sum(xr[j, :, cols].astype(F32) for j in range(4))
        zs[i] = total.astype(BF)
    keep(zs.at[z], zr.at[z], 9)

    @pl.loop(1, 8)
    def _(j):
        tz = (z + j) % 8
        send(zs.at[tz], zr.at[z], 17, 9, device(x, y, tz, c))

    wait(grecv.at[0], rsem.at[5])
    for h in range(HEADS):
        gv_out[:, h * HD : (h + 1) * HD] = grecv[0, h]
    stores[1].start()
    wait(grecv.at[1], rsem.at[6])

    @pl.loop(0, HEADS)
    def _(h):
        gk_out[:, lanes(h)] = turn(grecv[1, h], -1.0).astype(BF)

    stores[2].start()
    wait(zr, rsem.at[9])
    stores[4].start()
    wait(grecv.at[2], rsem.at[7])
    stores[3].start()

    for store in stores:
        store.wait()
    most = lambda ref: ref.at[pl.ds(0, 15)]
    for n in range(3):
        wait(rel.at[n, pl.ds(0, 7)], ssem.at[n])
        wait(rel.at[n], ssem.at[21 + n])
        wait(rel.at[n, pl.ds(0, 7)], ssem.at[24 + n])
    wait(most(gd), ssem.at[3])
    wait(most(gd), ssem.at[4])
    for n in range(3):
        wait(most(gsend.at[n]), ssem.at[5 + n])

    def weights_left(core, parts):
        wait(wbuf.at[parts, 0, pl.ds(0, 7), 0, 0], ssem.at[8])
        wait(wbuf.at[parts], ssem.at[13])
        wait(wbuf.at[parts, 0, :, 0, :], ssem.at[9])
        wait(wbuf.at[parts, 0, :, 0, 0], ssem.at[16])
        wait(wbuf.at[parts, 0], ssem.at[14])
        wait(wbuf.at[parts, 0, :, :, 0], ssem.at[15])

    per_core(weights_left)
    wait(zs.at[pl.ds(0, 7)], ssem.at[17])
    wait(ct.at[:, pl.ds(0, 4 * HD)], ssem.at[10])
    wait(ct.at[:, pl.ds(0, 3 * HD)], ssem.at[19])
    wait(at_all.at[pl.ds(0, 5 * ROWS)], ssem.at[11])
    wait(at_all.at[pl.ds(0, 2 * ROWS)], ssem.at[18])
    wait(gw_send.at[pl.ds(0, 3)], ssem.at[12])

    @pl.when(c != xh)
    def _():
        wait(gw_send.at[0], ssem.at[12])


def local(query, key_in, value, bucket, clip_cost, positions, out_weight, cotangent):
    _, _, axis_of, frequency = rotary_layout(HD)
    rates = np.zeros((8, HD), np.float32)
    rates[axis_of, np.arange(HD)] = frequency
    perm = jnp.asarray(partner_matrix(), BF)

    vmem = pl.BlockSpec(memory_space=pltpu.VMEM)
    smem = pl.BlockSpec(memory_space=pltpu.SMEM)
    bf = lambda *shape: pltpu.VMEM(shape, BF)
    f32 = lambda *shape: pltpu.VMEM(shape, F32)
    shape = jax.ShapeDtypeStruct
    hbm = pl.BlockSpec(memory_space=pl.ANY)
    table = shape((ROWS, HD), F32)
    rows = shape((ROWS, TOKENS), BF)
    mixed, grad_key, grad_value, raw_query, terms, cos, sin = pl.pallas_call(
        kernel,
        out_shape=(shape((ROWS, D), BF), rows, rows, shape((16, ROWS, HD), BF), shape((8, 192, HD), BF), table, table),
        in_specs=[hbm] * 3 + [vmem] * 3 + [hbm] * 2 + [smem] * 2,
        out_specs=(hbm,) * 7,
        scratch_shapes=[
            f32(ROWS, HD), f32(ROWS, HD),
            bf(ROWS, TOKENS), bf(ROWS, TOKENS), bf(ROWS, TOKENS), bf(ROWS, D),
            bf(ROWS, D), bf(ROWS, TOKENS), bf(ROWS, TOKENS),
            bf(3, 2, 8, ROWS, HD), bf(3, 8, ROWS, HD),
            bf(TOKENS, HD), bf(TOKENS, HD), bf(TOKENS, HD),
            bf(HD, TOKENS), bf(HD + 16, TOKENS),
            bf(PARTS, 2, 8, 4, 2, 16, WIDE),
            bf(TOKENS, TOKENS),
            f32(HD, TOKENS), f32(1, TOKENS),
            bf(TOKENS, HD), bf(TOKENS, HD),
            bf(2, ROWS, 1024),
            bf(16, HD, ROWS), bf(HD, TOKENS),
            bf(HD, TOKENS), f32(HD, TOKENS),
            bf(3, 16, ROWS, HD), bf(3, 16, ROWS, HD),
            bf(D, ROWS), bf(768, 1024), bf(1024, 1024),
            bf(4, 192, 1024), bf(4, 192, 1024),
            bf(8, 192, HD), bf(8, 192, HD),
            pltpu.SemaphoreType.DMA((27,)), pltpu.SemaphoreType.DMA((47,)), pltpu.SemaphoreType.DMA((11,)),
        ],
        compiler_params=pltpu.CompilerParams(
            collective_id=0, has_side_effects=True, vmem_limit_bytes=62 * 2**20
        ),
    )(
        query[0], key_in[0], value[0], positions, jnp.asarray(rates), perm,
        out_weight, cotangent[0], bucket, clip_cost,
    )
    mixed, grad_query, grad_key, grad_value, grad_weight = pl.pallas_call(
        finish,
        out_shape=(shape((ROWS, D), BF), rows, rows, rows, shape((192, HD), F32)),
        in_specs=[hbm] * 8,
        out_specs=(hbm,) * 5,
        scratch_shapes=[
            bf(ROWS, D), bf(ROWS, TOKENS), bf(ROWS, TOKENS), bf(16, ROWS, HD), bf(8, 192, HD),
            f32(ROWS, HD), f32(ROWS, HD), bf(HD, HD), bf(ROWS, TOKENS), f32(192, HD),
            pltpu.SemaphoreType.DMA((8,)), pltpu.SemaphoreType.DMA((5,)),
        ],
    )(mixed, grad_key, grad_value, raw_query, terms, cos, sin, perm)
    return mixed[None], grad_query[None], grad_key[None], grad_value[None], grad_weight.T


def solution(mesh):
    in_specs = (
        P("dp", "sp", None),
        P("dp", "sp", None),
        P("dp", "sp", None),
        P("dp"),
        P("dp", None),
        P(None, "dp", "sp"),
        P("sp", None),
        P("dp", "sp", None),
    )
    out_specs = (
        P("dp", "sp", None),
        P("dp", "sp", None),
        P("dp", "sp", None),
        P("dp", "sp", None),
        P("sp", "dp"),
    )
    return jax.shard_map(local, mesh=mesh, in_specs=in_specs, out_specs=out_specs, check_vma=False)
```

```python
import functools

import jax
import jax.numpy as jnp
import numpy as np
from jax import lax
from jax.experimental import pallas as pl
from jax.experimental.pallas import tpu as pltpu
from jax.sharding import PartitionSpec as P

MESH = pl.DeviceIdType.MESH
BF = jnp.bfloat16
F32 = jnp.float32

HD = 128
HEADS = 16
CLIPS = 4
ROWS = 128
TOKENS = 2048
SLOT = TOKENS // CLIPS
D = 3072
PARTS = 2
SPLIT = 1
WIDE = D // PARTS
QB = 256
LOG2E = 1.4426950408889634
FACTOR = HD ** (-0.5)
SCALE = FACTOR * LOG2E


def rotary_layout(head_dim):
    quarter = head_dim // 4
    rest_span = (head_dim - quarter) // 2
    part_spans = (quarter, rest_span, head_dim - quarter - rest_span)
    partner, signs, axis_of, frequency = [], [], [], []
    offset = 0
    for part_index in range(3):
        part_span = part_spans[part_index]
        half_span = part_span // 2
        for inner_dim in range(part_span):
            pair_index = inner_dim % half_span
            if inner_dim < half_span:
                partner.append(offset + inner_dim + half_span)
                signs.append(-1.0)
            else:
                partner.append(offset + inner_dim - half_span)
                signs.append(1.0)
            axis_of.append(part_index)
            frequency.append(10000.0 ** (-pair_index / half_span))
        offset += part_span
    return np.array(partner), np.array(signs), np.array(axis_of), np.array(frequency)


def partner_matrix():
    partner, signs, _, _ = rotary_layout(HD)
    matrix = np.zeros((HD, HD), np.float32)
    matrix[partner, np.arange(HD)] = signs
    return matrix


def nt(left, right):
    return lax.dot_general(left, right, (((1,), (1,)), ((), ())), preferred_element_type=F32)


def nn(left, right):
    return jnp.dot(left, right, preferred_element_type=F32)


def al(index, size):
    return pl.multiple_of(index, size)


def finish(
    mixed_hbm, gk_hbm, gv_hbm, raw_hbm, terms_hbm, cos_hbm, sin_hbm, perm_hbm,
    mixed_out, gq_out, gk_out, gv_out, gw_out,
    mixed, gk, gv, raw, terms, cos, sin, perm, gq, gw, load_sem, store_sem,
):
    pairs = (
        (raw_hbm, raw), (cos_hbm, cos), (sin_hbm, sin), (perm_hbm, perm), (terms_hbm, terms),
        (mixed_hbm, mixed), (gk_hbm, gk), (gv_hbm, gv),
    )
    loads = [pltpu.make_async_copy(src, dst, load_sem.at[i]) for i, (src, dst) in enumerate(pairs)]
    pairs = ((gq, gq_out), (gw, gw_out), (mixed, mixed_out), (gk, gk_out), (gv, gv_out))
    stores = [pltpu.make_async_copy(src, dst, store_sem.at[i]) for i, (src, dst) in enumerate(pairs)]
    for load in loads:
        load.start()
    for load in loads[:4]:
        load.wait()
    for h in range(HEADS):
        part = raw[h]
        turned = part.astype(F32) * cos[...] - nn(part, perm[...]) * sin[...]
        gq[:, h * HD : (h + 1) * HD] = turned.astype(BF)
    stores[0].start()
    for load, store in zip(loads[5:], stores[2:]):
        load.wait()
        store.start()
    loads[4].wait()
    gw[...] = sum(terms[i].astype(F32) for i in range(8))
    stores[1].start()
    for store in stores:
        store.wait()


def kernel(
    q_hbm, k_hbm, v_hbm, pos_ref, freq_ref, perm_ref, w_hbm, cot_hbm, bucket_ref, cost_ref,
    mixed_hbm, gk_hbm, gv_hbm, gq_hbm, zr_hbm, cos_hbm, sin_hbm,
    cos_ref, sin_ref,
    q_ref, k_ref, v_ref, cot_ref, mixed_out, gk_out, gv_out,
    rin, rel, qh, kh, vh, kt, vt, wbuf, probs, ot, rl, att, dealt, att_tok,
    gd, gdh, dot_t, dq_t, gsend, grecv, cot_t, ct, at_all, gw_send, xr, zs, zr,
    ssem, rsem, lsem,
):
    dp, sp = lax.axis_index("dp"), lax.axis_index("sp")
    y, xl, c = dp // 4, (dp // 2) % 2, dp % 2
    z, xh = sp // 2, sp % 2
    x = xh * 2 + xl

    def device(x_, y_, z_, c_):
        return (y_ * 4 + (x_ % 2) * 2 + c_, z_ * 2 + x_ // 2)

    def send(src, dst, s, r, to):
        pltpu.make_async_remote_copy(
            src_ref=src, dst_ref=dst, send_sem=ssem.at[s], recv_sem=rsem.at[r],
            device_id=to, device_id_type=MESH,
        ).start()

    def keep(src, dst, r):
        pltpu.make_async_copy(src, dst, rsem.at[r]).start()

    def wait(view, sem):
        pltpu.make_async_copy(view, view, sem).wait()

    loads = [
        pltpu.make_async_copy(src, dst, lsem.at[i])
        for i, (src, dst) in enumerate(((cot_hbm, cot_ref), (q_hbm, q_ref), (k_hbm, k_ref), (v_hbm, v_ref)))
    ]
    for load in loads:
        load.start()

    vt[HD:, :] = jnp.ones((16, TOKENS), BF)

    barrier = pltpu.get_barrier_semaphore()

    def greet(to):
        pl.semaphore_signal(barrier, inc=1, device_id=to, device_id_type=MESH)

    @pl.loop(1, 16)
    def _(j):
        greet((dp, lax.rem(sp + j, 16)))

    @pl.loop(1, 8)
    def _(j):
        greet(device(x, (y + j // 2) % 4, z, (c + j) % 2))
        greet(device((x + j // 2) % 4, y, z, (c + j) % 2))

    pl.semaphore_wait(barrier, 29)

    def per_core(run):
        @pl.when(c == 0)
        def _():
            run(0, pl.ds(0, SPLIT))

        @pl.when(c == 1)
        def _():
            run(1, pl.ds(SPLIT, PARTS - SPLIT))

    def give_piece(core, parts):
        for t in range(parts.start, parts.start + parts.size):
            piece = w_hbm.at[pl.ds(al((y * 2 + xl) * 16, 16), 16), pl.ds(t * WIDE, WIDE)]
            spot = wbuf.at[t, xh, z, y, xl]
            keep(piece, spot, 8)

            @pl.loop(1, 8)
            def _(j, piece=piece, spot=spot):
                send(piece, spot, 8, 8, device(x, y, (z + j) % 8, c))

    per_core(give_piece)

    lanes = lambda h: pl.ds(al(h * HD, HD), HD)
    sibling = device(x, y, z, 1 - c)
    me8 = y * 2 + c

    def hand_over_cotangent():
        for j in range(1, 4):
            view = ct.at[:, lanes((y + 4 - j) % 4 * 2 + c)]
            wait(view, rsem.at[36 + j])
            send(view, view, 19, 10, sibling)

    angles = sum(
        jnp.broadcast_to(pos_ref[a].astype(F32), (ROWS, ROWS)).T * freq_ref[a : a + 1] for a in range(3)
    )
    cos_ref[...] = jnp.cos(angles)
    sin_ref[...] = jnp.sin(angles)

    cos, sin, perm = cos_ref[...], sin_ref[...], perm_ref[...]

    def turn(block, direction):
        return block.astype(F32) * cos + direction * nn(block, perm) * sin

    mine = pl.ds(al(sp * ROWS, ROWS), ROWS)

    partner = (dp, z * 2 + 1 - xh)
    theirs = pl.ds(al(partner[1] * ROWS, ROWS), ROWS)

    def fill(n, src, side):
        @pl.loop(0, 8)
        def _(i):
            part = src[:, lanes(i * 2 + side)]
            rin[n, side, i] = part.T if n == 2 else turn(part, 1.0).astype(BF)

    def cross(n):
        send(rin.at[n, 1 - xh], rel.at[n], 21 + n, 44 + n, partner)

    def along(n, view, dst, rows, s, r):
        spot = dst.at[pl.ds(0, HD), rows] if n == 2 else dst.at[rows]
        keep(view.at[z], spot, r)

        @pl.loop(1, 8)
        def _(j):
            tz = lax.rem(z + j, 8)
            send(view.at[tz], spot, s, r, (dp, tz * 2 + xh))

    arrays = ((0, q_ref, qh), (1, k_ref, kh), (2, v_ref, vt))

    def hand_on(n, dst):
        wait(rel.at[n], rsem.at[44 + n])
        along(n, rel.at[n], dst, theirs, 24 + n, 47 if n == 2 else n)

    for n, src, _ in arrays[:2]:
        loads[1 + n].wait()
        fill(n, src, 1 - xh)
        cross(n)
    fill(0, q_ref, xh)
    along(0, rin.at[0, xh], qh, mine, 0, 0)

    loads[0].wait()
    for i in range(D // 128):
        cot_t[i * 128 : (i + 1) * 128, :] = cot_ref[:, i * 128 : (i + 1) * 128].T
    quarter = cot_t.at[pl.ds(al(y * 768, 768), 768)]
    keep(quarter, ct.at[:, lanes(me8)], 10)
    send(quarter, ct.at[:, lanes(me8)], 10, 10, sibling)
    for j in range(1, 4):
        ty = (y + j) % 4
        send(cot_t.at[pl.ds(al(ty * 768, 768), 768)], ct.at[:, lanes(me8)], 10, 36 + j, device(x, ty, z, c))

    fill(1, k_ref, xh)
    loads[3].wait()
    fill(2, v_ref, xh)
    fill(2, v_ref, 1 - xh)

    def at(core, i, k):
        return ((x + 8 + i) % 4, (y + 8 + k) % 4) if core else ((x + 8 + k) % 4, (y + 8 + i) % 4)

    def block(core, parts, i, k):
        bx, by = at(core, i, k)
        return wbuf.at[parts, bx // 2, :, by, bx % 2]

    def half_of(core, parts, i, k, m):
        bx, by = at(core, i, k)
        return wbuf.at[parts, bx // 2, pl.ds(4 * m, 4), by, bx % 2]

    def ring_to(core, i, k):
        return device(*at(core, i, k), z, c)

    order = (0, -1, 1, 2)

    def share(core, parts, n):
        view = block(core, parts, order[n], 0)
        send(view, view, 14, 21 + 4 * n, ring_to(core, 0, 1))
        send(view, view, 14, 22 + 4 * n, ring_to(core, 0, -1))
        send(view, view, 13, 13, sibling)

    def pass_on(n):
        def run(core, parts):
            for side, m in ((-1, 0), (1, 1)):
                view = block(core, parts, order[n], side)
                part = half_of(core, parts, order[n], side, m)
                wait(view, rsem.at[21 + 4 * n + m])
                send(part, part, 15, 23 + 4 * n + m, ring_to(core, 0, -side))
                send(view, view, 13, 13, sibling)

        per_core(run)

    def first_ring_start(core, parts):
        own = block(core, parts, 0, 0)
        wait(own, rsem.at[8])
        send(own, own, 9, 17, ring_to(core, 1, 0))
        send(own, own, 9, 18, ring_to(core, -1, 0))
        share(core, parts, 0)

    def first_ring(core, parts):
        for n, side, m in ((1, -1, 0), (2, 1, 1)):
            part = half_of(core, parts, side, 0, m)
            wait(block(core, parts, side, 0), rsem.at[17 + m])
            send(part, part, 16, 19 + m, ring_to(core, -side, 0))
            share(core, parts, n)

    def first_ring_end(core, parts):
        for m in range(2):
            wait(half_of(core, parts, 2, 0, m), rsem.at[19 + m])
        share(core, parts, 3)

    def second_ring_end(core, parts):
        for n in range(4):
            for m in range(2):
                wait(half_of(core, parts, order[n], 2, m), rsem.at[23 + 4 * n + m])
            view = block(core, parts, order[n], 2)
            send(view, view, 13, 13, sibling)

    def others_come(core, parts):
        rest = pl.ds(0, SPLIT) if core else pl.ds(SPLIT, PARTS - SPLIT)
        wait(wbuf.at[rest], rsem.at[13])

    per_core(first_ring_start)
    along(1, rin.at[1, xh], kh, mine, 1, 1)
    for n, _, dst in arrays[:2]:
        hand_on(n, dst)
    along(2, rin.at[2, xh], vt, mine, 2, 2)
    per_core(first_ring)
    cross(2)
    hand_over_cotangent()
    pass_on(0)
    per_core(first_ring_end)
    hand_on(2, vt)
    pass_on(1)

    wait(qh, rsem.at[0])
    wait(kh, rsem.at[1])
    narrow = jnp.where(bucket_ref[0] == 1, 0.0, -1e30).astype(F32)

    def weigh(b):
        cols = pl.ds(al(b * QB, QB), QB)
        slot = b // (SLOT // QB)
        scores = nt(kh[...], qh[cols, :])
        parts = [scores[i * SLOT : (i + 1) * SLOT] for i in range(CLIPS)]
        masks = [jnp.where(slot == i, 0.0, narrow) for i in range(CLIPS)]
        tops = [jnp.max(part, axis=0, keepdims=True) + mask for part, mask in zip(parts, masks)]
        top = functools.reduce(jnp.maximum, tops) * SCALE
        for i in range(CLIPS):
            low = jnp.exp2(parts[i] * SCALE - (top - masks[i])).astype(BF)
            probs[i * SLOT : (i + 1) * SLOT, cols] = low

    pl.loop(0, 4)(weigh)
    pass_on(2)
    pl.loop(4, TOKENS // QB)(weigh)

    def weighted(side, cols):
        spans = [lanes(i * 2 + side) for i in range(8)]
        left = jnp.concatenate([vt[:, span] for span in spans], axis=1)
        right = jnp.concatenate([probs[span, cols] for span in spans], axis=0)
        return nn(left, right)

    wait(vt.at[pl.ds(0, HD), pl.ds(0, 8 * HD)], rsem.at[2])

    @pl.loop(0, TOKENS // QB)
    def _(b):
        cols = pl.ds(al(b * QB, QB), QB)
        out = weighted(xh, cols)
        rl[:, cols] = out[HD : HD + 1]
        ot[:, cols] = out[:HD]

    pass_on(3)

    wait(vt.at[pl.ds(0, HD), pl.ds(0, 8 * HD)], rsem.at[47])

    @pl.loop(0, TOKENS // QB)
    def _(b):
        cols = pl.ds(al(b * QB, QB), QB)
        out = weighted(1 - xh, cols)
        scale = 1.0 / (rl[:, cols] + out[HD : HD + 1])
        rl[:, cols] = scale
        out = (ot[:, cols] + out[:HD]) * scale
        ot[:, cols] = out
        att[cols, :] = out.T.astype(BF)

    costs = [cost_ref[0, k] for k in range(CLIPS)]
    wide = bucket_ref[0] == 1
    rank = []
    for k in range(CLIPS):
        count = jnp.int32(0)
        for j in range(CLIPS):
            if j != k:
                above = costs[j] >= costs[k] if j < k else costs[j] > costs[k]
                count = count + jnp.where(above, 1, 0)
        rank.append(jnp.where(wide, k, count))
    choose = [[jnp.where(rank[k] == r, 1.0, 0.0).astype(F32) for k in range(CLIPS)] for r in range(CLIPS)]

    slots = [att[k * SLOT : (k + 1) * SLOT, :].astype(F32) for k in range(CLIPS)]
    for r in range(CLIPS):
        picked = sum(slots[k] * choose[r][k] for k in range(CLIPS))
        dealt[r * SLOT : (r + 1) * SLOT, :] = picked.astype(BF)

    here = att_tok.at[xh, :, lanes(z)]
    keep(dealt.at[mine], here, 3)

    @pl.loop(1, 16)
    def _(j):
        t = lax.rem(sp + j, 16)
        send(dealt.at[pl.ds(al(t * ROWS, ROWS), ROWS)], here, 3, 3, (dp, t))

    per_core(second_ring_end)

    per_core(others_come)

    def grad_of(h):
        total = sum(
            nt(wbuf[t, h % 2, h // 2].reshape(HD, WIDE), cot_ref[:, t * WIDE : (t + 1) * WIDE])
            for t in range(PARTS)
        )
        gd[h] = total.astype(BF)

    grad_of(sp)
    keep(gd.at[sp], gdh.at[:, mine], 4)

    @pl.loop(0, 15)
    def _(j):
        h = lax.rem(sp + 1 + lax.rem(j + 7, 15), 16)
        grad_of(h)
        send(gd.at[h], gdh.at[:, mine], 4, 4, (dp, h))

    wait(att_tok, rsem.at[3])
    def rows_of(ty, tc, first=0, count=ROWS):
        return at_all.at[pl.ds(al((ty * 2 + tc) * ROWS + first, count), count)]

    at_here = rows_of(y, c)
    keep(att_tok.at[c], at_here, 11)
    for tc in range(2):
        send(att_tok.at[tc], at_here, 11, 40 + c, device(x, (y + 1) % 4, z, tc))
        send(att_tok.at[tc], at_here, 11, 42 + c, device(x, (y + 3) % 4, z, tc))
    send(att_tok.at[1 - c], at_here, 11, 11, sibling)

    for t in range(PARTS):

        @pl.loop(0, WIDE // 512)
        def _(i, t=t):
            cols = pl.ds(al(i * 512, 512), 512)
            total = nn(att_tok[0], wbuf[t, 0, :, :, :, :, cols].reshape(1024, 512))
            total += nn(att_tok[1], wbuf[t, 1, :, :, :, :, cols].reshape(1024, 512))
            mixed_out[:, pl.ds(al(t * WIDE + i * 512, 512), 512)] = total.astype(BF)

    stores = [
        pltpu.make_async_copy(src, dst, lsem.at[4 + i])
        for i, (src, dst) in enumerate(
            (
                (mixed_out, mixed_hbm), (gv_out, gv_hbm), (gk_out, gk_hbm), (grecv.at[2], gq_hbm), (zr, zr_hbm),
                (cos_ref, cos_hbm), (sin_ref, sin_hbm),
            )

        )
    ]
    for store in (stores[0], stores[5], stores[6]):
        store.start()

    for m, step in ((0, 3), (1, 1)):
        ty = (y + step) % 4
        for tc in range(2):
            wait(rows_of(ty, tc), rsem.at[40 + 2 * m + tc])
            part = rows_of(ty, tc, 64 * m, 64)
            send(part, part, 18, 11, device(x, (y + 4 - step) % 4, z, c))

    kt[...] = kh[...].T
    vh[...] = vt[:HD, :].T

    wait(gdh, rsem.at[4])
    slots = [gdh[:, k * SLOT : (k + 1) * SLOT].astype(F32) for k in range(CLIPS)]
    for k in range(CLIPS):
        picked = sum(slots[r] * choose[r][k] for r in range(CLIPS))
        part = slice(k * SLOT, (k + 1) * SLOT)
        dot_t[:, part] = (picked * rl[:, part]).astype(BF)

    def give(n, t):
        @pl.when(t == sp)
        def _():
            keep(gsend.at[n, t], grecv.at[n, sp], 5 + n)

        @pl.when(t != sp)
        def _():
            send(gsend.at[n, t], grecv.at[n, sp], 5 + n, 5 + n, (dp, t))

    centre = jnp.sum(dot_t[...].astype(F32) * ot[...], axis=0, keepdims=True)

    @pl.loop(0, TOKENS // QB)
    def _(i):
        b = (i + sp // 2 + 4) % (TOKENS // QB)
        rows = pl.ds(al(b * QB, QB), QB)
        low = probs[rows, :]
        value_grad = nt(low, dot_t[...]).astype(BF)
        gsend[0, b * 2] = value_grad[:ROWS]
        gsend[0, b * 2 + 1] = value_grad[ROWS:]
        give(0, b * 2)
        give(0, b * 2 + 1)

    wait(ct.at[:, pl.ds(0, 5 * HD)], rsem.at[10])
    wait(at_all.at[pl.ds(0, 4 * ROWS)], rsem.at[11])
    for b in range(4):
        gw_send[b] = nn(ct[b * 192 : (b + 1) * 192, :], at_all[...]).astype(BF)
        tx, tc = 2 * c + b // 2, b % 2
        same = jnp.logical_and(tx == x, tc == c)

        @pl.when(same)
        def _(b=b):
            keep(gw_send.at[b], xr.at[x], 12)

        @pl.when(jnp.logical_not(same))
        def _(b=b, tx=tx, tc=tc):
            send(gw_send.at[b], xr.at[x], 12, 12, device(tx, y, z, tc))

    dq_t[...] = jnp.zeros_like(dq_t)

    @pl.loop(0, TOKENS // QB)
    def _(i):
        b = (i + sp // 2) % (TOKENS // QB)
        rows = pl.ds(al(b * QB, QB), QB)
        grad_probs = nn(vh[rows, :], dot_t[...])
        grad_scores = (probs[rows, :].astype(F32) * (grad_probs - centre)).astype(BF)
        key_grad = (nn(grad_scores, qh[...]) * FACTOR).astype(BF)
        gsend[1, b * 2] = key_grad[:ROWS]
        gsend[1, b * 2 + 1] = key_grad[ROWS:]
        give(1, b * 2)
        give(1, b * 2 + 1)
        dq_t[...] += nn(kt[:, rows], grad_scores)

    @pl.loop(0, HEADS)
    def _(i):
        t = lax.rem(sp + i, 16)
        gsend[2, t] = (dq_t[:, lanes(t)].T * FACTOR).astype(BF)
        give(2, t)

    wait(xr, rsem.at[12])
    for i in range(8):
        cols = slice(i * HD, (i + 1) * HD)
        total = sum(xr[j, :, cols].astype(F32) for j in range(4))
        zs[i] = total.astype(BF)
    keep(zs.at[z], zr.at[z], 9)

    @pl.loop(1, 8)
    def _(j):
        tz = (z + j) % 8
        send(zs.at[tz], zr.at[z], 17, 9, device(x, y, tz, c))

    wait(grecv.at[0], rsem.at[5])
    for h in range(HEADS):
        gv_out[:, h * HD : (h + 1) * HD] = grecv[0, h]
    stores[1].start()
    wait(grecv.at[1], rsem.at[6])

    @pl.loop(0, HEADS)
    def _(h):
        gk_out[:, lanes(h)] = turn(grecv[1, h], -1.0).astype(BF)

    stores[2].start()
    wait(zr, rsem.at[9])
    stores[4].start()
    wait(grecv.at[2], rsem.at[7])
    stores[3].start()

    for store in stores:
        store.wait()
    most = lambda ref: ref.at[pl.ds(0, 15)]
    for n in range(3):
        wait(rel.at[n, pl.ds(0, 7)], ssem.at[n])
        wait(rel.at[n], ssem.at[21 + n])
        wait(rel.at[n, pl.ds(0, 7)], ssem.at[24 + n])
    wait(most(gd), ssem.at[3])
    wait(most(gd), ssem.at[4])
    for n in range(3):
        wait(most(gsend.at[n]), ssem.at[5 + n])

    def weights_left(core, parts):
        wait(wbuf.at[parts, 0, pl.ds(0, 7), 0, 0], ssem.at[8])
        wait(wbuf.at[parts], ssem.at[13])
        wait(wbuf.at[parts, 0, :, 0, :], ssem.at[9])
        wait(wbuf.at[parts, 0, :, 0, 0], ssem.at[16])
        wait(wbuf.at[parts, 0], ssem.at[14])
        wait(wbuf.at[parts, 0, :, :, 0], ssem.at[15])

    per_core(weights_left)
    wait(zs.at[pl.ds(0, 7)], ssem.at[17])
    wait(ct.at[:, pl.ds(0, 4 * HD)], ssem.at[10])
    wait(ct.at[:, pl.ds(0, 3 * HD)], ssem.at[19])
    wait(at_all.at[pl.ds(0, 5 * ROWS)], ssem.at[11])
    wait(at_all.at[pl.ds(0, 2 * ROWS)], ssem.at[18])
    wait(gw_send.at[pl.ds(0, 3)], ssem.at[12])

    @pl.when(c != xh)
    def _():
        wait(gw_send.at[0], ssem.at[12])


def local(query, key_in, value, bucket, clip_cost, positions, out_weight, cotangent):
    _, _, axis_of, frequency = rotary_layout(HD)
    rates = np.zeros((8, HD), np.float32)
    rates[axis_of, np.arange(HD)] = frequency
    perm = jnp.asarray(partner_matrix(), BF)

    vmem = pl.BlockSpec(memory_space=pltpu.VMEM)
    smem = pl.BlockSpec(memory_space=pltpu.SMEM)
    bf = lambda *shape: pltpu.VMEM(shape, BF)
    f32 = lambda *shape: pltpu.VMEM(shape, F32)
    shape = jax.ShapeDtypeStruct
    hbm = pl.BlockSpec(memory_space=pl.ANY)
    table = shape((ROWS, HD), F32)
    rows = shape((ROWS, TOKENS), BF)
    mixed, grad_key, grad_value, raw_query, terms, cos, sin = pl.pallas_call(
        kernel,
        out_shape=(shape((ROWS, D), BF), rows, rows, shape((16, ROWS, HD), BF), shape((8, 192, HD), BF), table, table),
        in_specs=[hbm] * 3 + [vmem] * 3 + [hbm] * 2 + [smem] * 2,
        out_specs=(hbm,) * 7,
        scratch_shapes=[
            f32(ROWS, HD), f32(ROWS, HD),
            bf(ROWS, TOKENS), bf(ROWS, TOKENS), bf(ROWS, TOKENS), bf(ROWS, D),
            bf(ROWS, D), bf(ROWS, TOKENS), bf(ROWS, TOKENS),
            bf(3, 2, 8, ROWS, HD), bf(3, 8, ROWS, HD),
            bf(TOKENS, HD), bf(TOKENS, HD), bf(TOKENS, HD),
            bf(HD, TOKENS), bf(HD + 16, TOKENS),
            bf(PARTS, 2, 8, 4, 2, 16, WIDE),
            bf(TOKENS, TOKENS),
            f32(HD, TOKENS), f32(1, TOKENS),
            bf(TOKENS, HD), bf(TOKENS, HD),
            bf(2, ROWS, 1024),
            bf(16, HD, ROWS), bf(HD, TOKENS),
            bf(HD, TOKENS), f32(HD, TOKENS),
            bf(3, 16, ROWS, HD), bf(3, 16, ROWS, HD),
            bf(D, ROWS), bf(768, 1024), bf(1024, 1024),
            bf(4, 192, 1024), bf(4, 192, 1024),
            bf(8, 192, HD), bf(8, 192, HD),
            pltpu.SemaphoreType.DMA((27,)), pltpu.SemaphoreType.DMA((48,)), pltpu.SemaphoreType.DMA((11,)),
        ],
        compiler_params=pltpu.CompilerParams(
            collective_id=0, has_side_effects=True, vmem_limit_bytes=62 * 2**20
        ),
    )(
        query[0], key_in[0], value[0], positions, jnp.asarray(rates), perm,
        out_weight, cotangent[0], bucket, clip_cost,
    )
    mixed, grad_query, grad_key, grad_value, grad_weight = pl.pallas_call(
        finish,
        out_shape=(shape((ROWS, D), BF), rows, rows, rows, shape((192, HD), F32)),
        in_specs=[hbm] * 8,
        out_specs=(hbm,) * 5,
        scratch_shapes=[
            bf(ROWS, D), bf(ROWS, TOKENS), bf(ROWS, TOKENS), bf(16, ROWS, HD), bf(8, 192, HD),
            f32(ROWS, HD), f32(ROWS, HD), bf(HD, HD), bf(ROWS, TOKENS), f32(192, HD),
            pltpu.SemaphoreType.DMA((8,)), pltpu.SemaphoreType.DMA((5,)),
        ],
    )(mixed, grad_key, grad_value, raw_query, terms, cos, sin, perm)
    return mixed[None], grad_query[None], grad_key[None], grad_value[None], grad_weight.T


def solution(mesh):
    in_specs = (
        P("dp", "sp", None),
        P("dp", "sp", None),
        P("dp", "sp", None),
        P("dp"),
        P("dp", None),
        P(None, "dp", "sp"),
        P("sp", None),
        P("dp", "sp", None),
    )
    out_specs = (
        P("dp", "sp", None),
        P("dp", "sp", None),
        P("dp", "sp", None),
        P("dp", "sp", None),
        P("sp", "dp"),
    )
    return jax.shard_map(local, mesh=mesh, in_specs=in_specs, out_specs=out_specs, check_vma=False)
```
